768 devices in a mesh: graph: 48 (over x, z), feat: 16 (over y, core).
Axes of the slice: x: 4, y: 8, z: 12, core: 2. Of those that a mesh axis runs over, the one named last changes fastest.
Arguments:
- feats: bfloat16 [256, 49152], P('feat', 'graph'), may hold values from -6 to 6
- w_self: bfloat16 [256, 256], P('feat'), may hold values from -0.25 to 0.25
- w_neigh: bfloat16 [256, 256], P('feat'), may hold values from -0.25 to 0.25
- bias: float32 [256], P('feat'), may hold values from -1 to 1
- cotangent: bfloat16 [256, 49152], P('feat', 'graph'), may hold values from -6 to 6
- block_ids: int32 [48, 48, 2], P('graph'), may hold values from 0 to 7
- req_counts: int32 [48, 48], P('graph'), may hold values from 1 to 2, as said below
- tile_dst: int32 [48, 48, 2], P('graph'), may hold values from 0 to 7
- adjacency: bfloat16 [48, 48, 2, 128, 128], P('graph'), may hold values from 0 to 1.5, as said below
Outputs:
- output: bfloat16 [256, 49152], P('feat', 'graph')
- feat_grad: float32 [256, 49152], P('feat', 'graph')
The draws below stay inside these ranges and needn't reach their ends.
Inputs may be any that keep to these rules, and one draw needn't show every extreme that they name: req_counts[p, p] = 2 for every part p. `adjacency`: each entry is 0 or an edge weight of 0.5 to 1.5; tiles of slots at or beyond req_counts hold entries too.
All inputs are finite; a program needn't handle non-finite values.
Results may differ from the reference program's by a relative error of at most 0.0035.
Values may be sent and summed in bfloat16 or wider, within the bound.
No kernel may reach another device: no remote copies, remote signals or barrier semaphores. Data moves between devices by JAX's collectives and lax.ppermute only.
A program may use at most 32 MiB of HBM per device.

```python
import math
import jax
import jax.numpy as jnp
import numpy as np
from jax import lax

H = 256
BLK = 128
NB = 8
CAP = 2
PARTS_SIZE = 48
NODES = 49152


def draw_req_counts(key, part):
    key = jax.random.fold_in(key, 11)
    values = jax.random.randint(key, (PARTS_SIZE, PARTS_SIZE), 1, CAP + 1)
    diagonal = jnp.arange(PARTS_SIZE)[:, None] == jnp.arange(PARTS_SIZE)[None, :]
    return jnp.where(diagonal, CAP, values).astype(jnp.int32)


def draw_adjacency(key, part):
    key = jax.random.fold_in(key, 23)
    key_rate, key_edge, key_weight = jax.random.split(key, 3)
    shape = (PARTS_SIZE, PARTS_SIZE, CAP, BLK, BLK)
    log_rate = jax.random.uniform(key_rate, (PARTS_SIZE, 1, 1, 1, BLK), jnp.float32, math.log(1.0 / 4096.0), math.log(1.0 / 8.0))
    edges = jax.random.uniform(key_edge, shape, jnp.float32) < jnp.exp(log_rate)
    weights = jax.random.uniform(key_weight, shape, jnp.float32, 0.5, 1.5)
    return (edges.astype(jnp.float32) * weights).astype(jnp.bfloat16)


def with_ends(array, stream_key, low, high):
    longest = array.shape.index(max(array.shape))
    spots = []
    for shift in (0, 1):
        where = [jax.random.randint(jax.random.fold_in(stream_key, axis), (), 0, length) for axis, length in enumerate(array.shape)]
        where[longest] = (where[longest] + shift) % array.shape[longest]
        spots.append(tuple(where))
    return array.at[spots[0]].set(low).at[spots[1]].set(high)


def block_scale(key, dims, shards, low, high):
    def one(dim, parts):
        heights = jax.random.uniform(jax.random.fold_in(jax.random.fold_in(key, 6), dim), (parts,), jnp.float32, low / len(shards), high / len(shards))
        return jnp.repeat(jnp.exp(heights), dims[dim] // parts).reshape((-1,) + (1,) * (len(dims) - dim - 1))

    factor_of = one(*shards[0])
    for cut in shards[1:]:
        factor_of = factor_of * one(*cut)
    return factor_of


def cumulative_ranks(count, lean):
    loads = [(1 << 20) // math.isqrt(rank ** lean) + 1 for rank in range(1, count + 1)]
    deviation = 1 + sum(loads) // (1 << 30)
    return np.cumsum(np.array([max(1, weight // deviation) for weight in loads]))


def ranked_ids(stream_key, extent, amount, lean):
    table = cumulative_ranks(amount, lean)
    pick = jax.random.randint(jax.random.fold_in(stream_key, 1), extent, 0, int(table[amount - 1]))
    rank = jnp.searchsorted(jnp.asarray(table, jnp.int32), pick, side="right")
    return jax.random.permutation(jax.random.fold_in(stream_key, 2), amount)[rank].astype(jnp.int32)


def scatter_about(own_key, shape, width, limit, shards=(), kind=jnp.bfloat16):
    result = jax.random.normal(own_key, shape, jnp.float32) * width
    if len(shards) > 0:
        result = block_scale(own_key, shape, shards, -0.22, 0.18) * result
    return jnp.clip(result, min=-limit, max=limit).astype(kind)


def setup_inputs(seed: int = 0) -> dict:
    seeds = jax.random.split(jax.random.key(seed), 10)
    return {
        "feats": scatter_about(seeds[0], (H, NODES), 1.0, 6.0, ((0, 16), (1, 48))),
        "w_self": scatter_about(seeds[1], (H, H), (2 * H) ** -0.5, 0.25, ((0, 16),)),
        "w_neigh": scatter_about(seeds[2], (H, H), (2 * H) ** -0.5, 0.25, ((0, 16),)),
        "bias": jnp.clip(jax.random.uniform(seeds[3], (H,), jnp.float32, -1.0, 1.0) * block_scale(seeds[3], (H,), ((0, 16),), -0.4, 0.0), -1.0, 1.0),
        "cotangent": scatter_about(seeds[4], (H, NODES), 1.0, 6.0, ((0, 16), (1, 48))),
        "block_ids": with_ends(ranked_ids(seeds[5], (PARTS_SIZE, PARTS_SIZE, CAP), NB, 2), jax.random.fold_in(seeds[5], 3), 0, NB - 1).astype(jnp.int32),
        "req_counts": draw_req_counts(jax.random.fold_in(seeds[9], 71), 0),
        "tile_dst": with_ends(jax.random.randint(seeds[7], (PARTS_SIZE, PARTS_SIZE, CAP), 0, NB), jax.random.fold_in(seeds[7], 1), 0, NB - 1).astype(jnp.int32),
        "adjacency": draw_adjacency(jax.random.fold_in(seeds[9], 71), 0),
    }


def tile_setup(part, block_ids, req_counts, tile_dst, adjacency):
    slot_ids = jnp.arange(CAP, dtype=jnp.int32)
    block_range = jnp.arange(NB, dtype=jnp.int32)
    live_mask = (slot_ids[None, :] < req_counts[part][:, None]).astype(jnp.float32)
    tile_vals = adjacency[part].astype(jnp.float32) * live_mask[:, :, None, None]
    dst_hot = (tile_dst[part][:, :, None] == block_range[None, None, :]).astype(jnp.float32)
    src_hot = (block_ids[part][:, :, None] == block_range[None, None, :]).astype(jnp.float32)
    return tile_vals, dst_hot, src_hot


def reference(feats, w_self, w_neigh, bias, cotangent, block_ids, req_counts, tile_dst, adjacency):
    highest = lax.Precision.HIGHEST
    slab_len = NB * BLK
    blocks = feats.reshape(H, PARTS_SIZE, NB, BLK)
    owners = jnp.arange(PARTS_SIZE, dtype=jnp.int32)

    def aggregate(part):
        tile_vals, dst_hot, src_hot = tile_setup(part, block_ids, req_counts, tile_dst, adjacency)
        fetched = blocks[:, owners[:, None], block_ids[part], :].astype(jnp.float32)
        contrib = jnp.einsum("hgci,gcij->hgcj", fetched, tile_vals, precision=highest)
        raw_sums = jnp.einsum("hgcj,gcn->hnj", contrib, dst_hot, precision=highest)
        degree = jnp.einsum("gcij,gcn->nj", tile_vals, dst_hot, precision=highest)
        inverse = 1.0 / jnp.maximum(degree, 1.0)
        aggregated = (raw_sums * inverse[None]).astype(jnp.bfloat16)
        return aggregated.reshape(H, slab_len), inverse.reshape(slab_len)

    agg_parts, inv_parts = lax.map(aggregate, owners)
    aggregated = jnp.transpose(agg_parts, (1, 0, 2)).reshape(H, PARTS_SIZE * slab_len)
    inverse = inv_parts.reshape(PARTS_SIZE * slab_len)
    preact = (jnp.dot(w_self.T, feats, preferred_element_type=jnp.float32)
              + jnp.dot(w_neigh.T, aggregated, preferred_element_type=jnp.float32)
              + bias[:, None])
    sigmoid_pre = jax.nn.sigmoid(preact)
    output = (preact * sigmoid_pre).astype(jnp.bfloat16)
    d_preact = (cotangent.astype(jnp.float32)
                * (sigmoid_pre + preact * sigmoid_pre * (1.0 - sigmoid_pre))).astype(jnp.bfloat16)
    self_grad = jnp.dot(w_self, d_preact, preferred_element_type=jnp.float32)
    scaled_grad = (jnp.dot(w_neigh, d_preact, preferred_element_type=jnp.float32)
                   * inverse[None]).astype(jnp.bfloat16)

    def give_back(running, part):
        tile_vals, dst_hot, src_hot = tile_setup(part, block_ids, req_counts, tile_dst, adjacency)
        own_grad = lax.dynamic_slice_in_dim(scaled_grad, part * slab_len, slab_len, 1)
        own_grad = own_grad.reshape(H, NB, BLK).astype(jnp.float32)
        chosen = jnp.einsum("hnj,gcn->hgcj", own_grad, dst_hot, precision=highest)
        tile_grads = jnp.einsum("hgcj,gcij->hgci", chosen, tile_vals, precision=highest)
        return running + jnp.einsum("hgci,gcn->hgni", tile_grads, src_hot, precision=highest), None

    running, _ = lax.scan(give_back, jnp.zeros((H, PARTS_SIZE, NB, BLK), jnp.float32), owners)
    feat_grad = self_grad + running.reshape(H, PARTS_SIZE * slab_len)
    return output, feat_grad
```

```python
import jax
import jax.numpy as jnp
from jax import lax
from jax.experimental import pallas as pl
from jax.experimental.pallas import tpu as pltpu
from jax.sharding import PartitionSpec as P

BLK = 128
NB = 8
CAP = 2
CHUNK = 8
VMEM_LIMIT = 24 * 1024 * 1024

SMEM_SPEC = pl.BlockSpec(memory_space=pltpu.SMEM)
VMEM_SPEC = pl.BlockSpec(memory_space=pltpu.VMEM)


def chunk_of(tiles):
    return CHUNK if tiles % CHUNK == 0 else CAP


def select_kernel(ids_ref, feats_ref, out_ref):
    for t in range(out_ref.shape[0]):
        start = pl.multiple_of(ids_ref[t] * BLK, BLK)
        out_ref[t] = feats_ref[:, pl.ds(start, BLK)]


def aggregate_kernel(dst_ref, counts_ref, fetched_ref, adj_ref, agg_ref, inv_ref):
    tiles, rows, _ = fetched_ref.shape
    chunk = chunk_of(tiles)
    row_ids = lax.broadcasted_iota(jnp.int32, (16, BLK), 0)
    zero = jnp.zeros((rows, BLK), jnp.bfloat16)

    def step(k, acc):
        columns = []
        for i in range(chunk):
            t = k * chunk + i
            live = (i % CAP) < counts_ref[t // CAP]
            dst = jnp.where(live, dst_ref[t], NB)
            block = fetched_ref[t]
            pieces = [jnp.where(dst == n, block, zero) for n in range(NB)]
            pieces.append((row_ids == dst).astype(jnp.float32).astype(jnp.bfloat16))
            columns.append(jnp.concatenate(pieces, axis=0))
        lhs = jnp.concatenate(columns, axis=1)
        start = pl.multiple_of(k * (chunk * BLK), chunk * BLK)
        weights = adj_ref[pl.ds(start, chunk * BLK), :]
        return acc + jnp.dot(lhs, weights, preferred_element_type=jnp.float32)

    acc = lax.fori_loop(
        0, tiles // chunk, step, jnp.zeros((NB * rows + 16, BLK), jnp.float32)
    )
    inverse = 1.0 / jnp.maximum(acc[NB * rows : NB * rows + NB], 1.0)
    inv_ref[...] = inverse
    for n in range(NB):
        part = acc[n * rows : (n + 1) * rows] * inverse[n : n + 1]
        agg_ref[:, n * BLK : (n + 1) * BLK] = part.astype(jnp.bfloat16)


def update_kernel(
    first_ref,
    dst_ref,
    counts_ref,
    agg_ref,
    bundle_ref,
    w_self_ref,
    w_neigh_ref,
    inv_ref,
    adj_ref,
    out_ref,
    self_ref,
    grads_ref,
    out_all,
    scaled,
):
    hidden, slab = agg_ref.shape
    rows = w_self_ref.shape[0]
    tiles = grads_ref.shape[0]
    chunk = chunk_of(tiles)
    weights = 2 * slab
    tail = bundle_ref[:, weights + 2 * hidden : weights + 2 * hidden + BLK].astype(jnp.float32)
    bias = tail[:, 0:1] + tail[:, 1:2] + tail[:, 2:3]
    w_self_all = bundle_ref[:, weights : weights + hidden]
    w_neigh_all = bundle_ref[:, weights + hidden : weights + 2 * hidden]
    contract_rows = (((0,), (0,)), ((), ()))
    width = 2 * BLK
    for start in range(0, slab, width):
        columns = slice(start, start + width)
        preact = (
            lax.dot_general(
                w_self_all, bundle_ref[:, columns], contract_rows, preferred_element_type=jnp.float32
            )
            + lax.dot_general(
                w_neigh_all, agg_ref[:, columns], contract_rows, preferred_element_type=jnp.float32
            )
            + bias
        )
        s = 1.0 / (1.0 + jnp.exp(-preact))
        silu = preact * s
        out_all[:, columns] = silu.astype(jnp.bfloat16)
        cotangent = bundle_ref[:, slab + start : slab + start + width].astype(jnp.float32)
        d_preact = (cotangent * (s + silu * (1.0 - s))).astype(jnp.bfloat16)
        self_ref[:, columns] = jnp.dot(
            w_self_ref[...], d_preact, preferred_element_type=jnp.float32
        )
        neigh = jnp.dot(w_neigh_ref[...], d_preact, preferred_element_type=jnp.float32)
        for half in range(width // BLK):
            n = start // BLK + half
            part = neigh[:, half * BLK : (half + 1) * BLK] * inv_ref[n : n + 1]
            scaled[n] = part.astype(jnp.bfloat16)
    out_ref[...] = out_all[pl.ds(pl.multiple_of(first_ref[0], rows), rows), :]

    zero = jnp.zeros((rows, BLK), jnp.bfloat16)
    contract_columns = (((1,), (1,)), ((), ()))

    def step(k, carry):
        for i in range(chunk):
            t = k * chunk + i
            live = (i % CAP) < counts_ref[t // CAP]
            chosen = jnp.where(live, scaled[dst_ref[t]], zero)
            start = pl.multiple_of(t * BLK, BLK)
            grads = lax.dot_general(
                chosen,
                adj_ref[pl.ds(start, BLK), :],
                contract_columns,
                preferred_element_type=jnp.float32,
            )
            grads_ref[t] = grads.astype(jnp.bfloat16)
        return carry

    lax.fori_loop(0, tiles // chunk, step, 0)


def sum_kernel(ids_ref, grads_ref, self_ref, out_ref):
    tiles, rows, _ = grads_ref.shape

    def step(t, sums):
        block = grads_ref[t].astype(jnp.float32)
        return tuple(
            total + jnp.where(ids_ref[t] == n, block, 0.0) for n, total in enumerate(sums)
        )

    start = tuple(self_ref[:, n * BLK : (n + 1) * BLK] for n in range(NB))
    sums = lax.fori_loop(0, tiles, step, start, unroll=4)
    for n in range(NB):
        out_ref[:, n * BLK : (n + 1) * BLK] = sums[n]


def params():
    return pltpu.CompilerParams(vmem_limit_bytes=VMEM_LIMIT)


def per_device(feats, w_self, w_neigh, bias, cotangent, block_ids, req_counts, tile_dst, adjacency):
    graph_parts = lax.axis_size("graph")
    hidden = w_self.shape[1]
    rows, slab = feats.shape
    tiles = graph_parts * CAP
    adj = adjacency.reshape(tiles * BLK, BLK)
    dst = tile_dst.reshape(tiles)
    counts = req_counts.reshape(graph_parts)
    first_row = (lax.axis_index("feat") * rows).astype(jnp.int32).reshape(1)

    high = lax.reduce_precision(bias, 8, 7)
    middle = lax.reduce_precision(bias - high, 8, 7)
    low = bias - high - middle
    terms = jnp.stack([high, middle, low], axis=1).astype(jnp.bfloat16)
    terms = jnp.pad(terms, ((0, 0), (0, BLK - 3)))
    bundle = jnp.concatenate([feats, cotangent, w_self, w_neigh, terms], axis=1)
    bundle = lax.all_gather(bundle, "feat", axis=0, tiled=True)

    asked = lax.all_to_all(block_ids[0], "graph", 0, 0).reshape(tiles)
    picked = pl.pallas_call(
        select_kernel,
        out_shape=jax.ShapeDtypeStruct((tiles, rows, BLK), jnp.bfloat16),
        in_specs=[SMEM_SPEC, VMEM_SPEC],
        out_specs=VMEM_SPEC,
        compiler_params=params(),
        name="select_blocks",
    )(asked, feats)
    fetched = lax.all_to_all(
        picked.reshape(graph_parts, CAP, rows, BLK), "graph", 0, 0
    ).reshape(tiles, rows, BLK)
    agg, inverse = pl.pallas_call(
        aggregate_kernel,
        out_shape=(
            jax.ShapeDtypeStruct((rows, slab), jnp.bfloat16),
            jax.ShapeDtypeStruct((NB, BLK), jnp.float32),
        ),
        in_specs=[SMEM_SPEC, SMEM_SPEC, VMEM_SPEC, VMEM_SPEC],
        out_specs=(VMEM_SPEC, VMEM_SPEC),
        compiler_params=params(),
        name="aggregate",
    )(dst, counts, fetched, adj)
    agg_all = lax.all_gather(agg, "feat", axis=0, tiled=True)
    output, self_grad, grads = pl.pallas_call(
        update_kernel,
        out_shape=(
            jax.ShapeDtypeStruct((rows, slab), jnp.bfloat16),
            jax.ShapeDtypeStruct((rows, slab), jnp.float32),
            jax.ShapeDtypeStruct((tiles, rows, BLK), jnp.bfloat16),
        ),
        in_specs=[SMEM_SPEC] * 3 + [VMEM_SPEC] * 6,
        out_specs=(VMEM_SPEC,) * 3,
        scratch_shapes=[
            pltpu.VMEM((hidden, slab), jnp.bfloat16),
            pltpu.VMEM((NB, rows, BLK), jnp.bfloat16),
        ],
        compiler_params=params(),
        name="update",
    )(first_row, dst, counts, agg_all, bundle, w_self, w_neigh, inverse, adj)
    returned = lax.all_to_all(
        grads.reshape(graph_parts, CAP, rows, BLK), "graph", 0, 0
    ).reshape(tiles, rows, BLK)
    feat_grad = pl.pallas_call(
        sum_kernel,
        out_shape=jax.ShapeDtypeStruct((rows, slab), jnp.float32),
        in_specs=[SMEM_SPEC, VMEM_SPEC, VMEM_SPEC],
        out_specs=VMEM_SPEC,
        compiler_params=params(),
        name="sum_returned",
    )(asked, returned, self_grad)
    return (output, feat_grad)


def solution(mesh):
    in_specs = (
        P("feat", "graph"),
        P("feat", None),
        P("feat", None),
        P("feat"),
        P("feat", "graph"),
        P("graph", None, None),
        P("graph", None),
        P("graph", None, None),
        P("graph", None, None, None, None),
    )
    out_specs = (P("feat", "graph"), P("feat", "graph"))
    return jax.shard_map(
        per_device, mesh=mesh, in_specs=in_specs, out_specs=out_specs, check_vma=False
    )
```

```python
import jax
import jax.numpy as jnp
from jax import lax
from jax.experimental import pallas as pl
from jax.experimental.pallas import tpu as pltpu
from jax.sharding import Mesh, PartitionSpec as P

BLK = 128
NB = 8
CAP = 2
VMEM_LIMIT = 24 * 1024 * 1024

SMEM = pl.BlockSpec(memory_space=pltpu.SMEM)
VMEM = pl.BlockSpec(memory_space=pltpu.VMEM)
HBM = pl.BlockSpec(memory_space=pltpu.HBM)

f32 = jnp.float32
bf16 = jnp.bfloat16


def chunk_of(tiles):
    return 8 if tiles % 8 == 0 else tiles


def prepare_kernel(
    ids_hbm,
    bias_hbm,
    feats_hbm,
    cot_hbm,
    w_self_hbm,
    w_neigh_hbm,
    slab_ref,
    ask_ref,
    bundle_ref,
    pad,
    ids_ref,
    bias_ref,
    sems,
):
    rows, slab = feats_hbm.shape
    parts = ids_hbm.shape[1]
    hidden = w_self_hbm.shape[1]
    ends = (0, slab, 2 * slab, 2 * slab + hidden, 2 * slab + 2 * hidden)
    pieces = [bundle_ref.at[:, pl.ds(i, j - i)] for i, j in zip(ends, ends[1:])]
    sources = (ids_hbm, bias_hbm, feats_hbm, feats_hbm, cot_hbm, w_self_hbm, w_neigh_hbm)
    targets = [ids_ref, bias_ref, slab_ref.at[:, pl.ds(0, slab)]] + pieces
    copies = [
        pltpu.make_async_copy(source, target, sems.at[i])
        for i, (source, target) in enumerate(zip(sources, targets))
    ]
    for copy in copies:
        copy.start()
    pad[...] = jnp.zeros_like(pad)
    copies[0].wait()
    pad[0:CAP, 0:parts] = ids_ref[...]
    for i in range(ask_ref.shape[0]):
        ask_ref[i] = pad[0:CAP, :]
    row = lax.broadcasted_iota(jnp.int32, (rows, BLK), 0)
    mine = row == lax.axis_index("z")
    for c in range(CAP):
        ids = jnp.broadcast_to(pad[c : c + 1, :], (rows, BLK))
        plane = jnp.where(mine, ids, 0).astype(f32).astype(bf16)
        slab_ref[:, slab + c * BLK : slab + (c + 1) * BLK] = plane
    copies[1].wait()
    wide = jnp.broadcast_to(bias_ref[...], (rows, rows))
    place = lax.broadcasted_iota(jnp.int32, (rows, rows), 0)
    place = place == lax.broadcasted_iota(jnp.int32, (rows, rows), 1)
    bias = jnp.sum(jnp.where(place, wide, 0.0), axis=1, keepdims=True)
    high = bias.astype(bf16).astype(f32)
    middle = (bias - high).astype(bf16).astype(f32)
    low = bias - high - middle
    lane = lax.broadcasted_iota(jnp.int32, (rows, BLK), 1)
    terms = jnp.where(lane == 0, high, jnp.where(lane == 1, middle, jnp.where(lane == 2, low, 0.0)))
    bundle_ref[:, ends[-1] :] = terms.astype(bf16)
    for copy in copies[2:]:
        copy.wait()


def select_kernel(ask_ref, slabs_ref, out_ref):
    along, _, rows, _ = out_ref.shape
    column = slabs_ref.shape[0]
    slab = NB * BLK
    first = lax.axis_index("x") * column
    for i in range(along):
        for k in range(column):
            for c in range(CAP):
                start = pl.multiple_of(ask_ref[i, c, first + k] * BLK, BLK)
                out_ref[i, k * CAP + c] = slabs_ref[k, :, pl.ds(start, BLK)]
    for c in range(CAP):
        plane = jnp.zeros((rows, BLK), f32)
        for k in range(column):
            plane += slabs_ref[k, :, slab + c * BLK : slab + (c + 1) * BLK].astype(f32)
        for i in range(along):
            out_ref[i, column * CAP + c] = plane.astype(bf16)


def tile_copies(adj_ref, adj, sems, step):
    return [
        pltpu.make_async_copy(
            adj_ref.at[pl.ds(k * step, step)], adj.at[pl.ds(k * step, step)], sems.at[k]
        )
        for k in range(adj_ref.shape[0] // step)
    ]


def wait_tiles(adj_ref, adj, sems, step, k):
    part = pl.ds(pl.multiple_of(k * step, step), step)
    pltpu.make_async_copy(adj_ref.at[part], adj.at[part], sems.at[k]).wait()


def aggregate_kernel(
    dst_hbm, counts_hbm, fetched_ref, adj_ref, agg_ref, inv_hbm, dst_ref, counts_ref, inv, adj, sems, small
):
    along, slots, rows, _ = fetched_ref.shape
    per_row = slots - CAP
    chunk = chunk_of(per_row)
    step_rows = chunk * BLK
    dst_copy = pltpu.make_async_copy(dst_hbm, dst_ref, small.at[0])
    counts_copy = pltpu.make_async_copy(counts_hbm, counts_ref, small.at[1])
    dst_copy.start()
    counts_copy.start()
    for copy in tile_copies(adj_ref, adj, sems, step_rows):
        copy.start()
    row_ids = lax.broadcasted_iota(jnp.int32, (16, BLK), 0)
    zero = jnp.zeros((rows, BLK), bf16)
    chunks = per_row // chunk
    dst_copy.wait()
    counts_copy.wait()

    def step(k, acc):
        columns = []
        for i in range(chunk):
            q = k * (chunk // CAP) + i // CAP
            live = (i % CAP) < counts_ref[0, q]
            dst = jnp.where(live, dst_ref[i % CAP, q], NB)
            block = fetched_ref[k // chunks, (k % chunks) * chunk + i]
            pieces = [jnp.where(dst == n, block, zero) for n in range(NB)]
            pieces.append((row_ids == dst).astype(f32).astype(bf16))
            columns.append(jnp.concatenate(pieces, axis=0))
        lhs = jnp.concatenate(columns, axis=1)
        wait_tiles(adj_ref, adj, sems, step_rows, k)
        weights = adj[pl.ds(pl.multiple_of(k * step_rows, step_rows), step_rows), :]
        return acc + jnp.dot(lhs, weights, preferred_element_type=f32)

    acc = lax.fori_loop(0, along * chunks, step, jnp.zeros((NB * rows + 16, BLK), f32))
    inverse = 1.0 / jnp.maximum(acc[NB * rows : NB * rows + NB], 1.0)
    inv[...] = inverse
    inv_copy = pltpu.make_async_copy(inv, inv_hbm, small.at[2])
    inv_copy.start()
    for n in range(NB):
        part = acc[n * rows : (n + 1) * rows] * inverse[n : n + 1]
        agg_ref[:, n * BLK : (n + 1) * BLK] = part.astype(bf16)
    inv_copy.wait()


def update_kernel(
    dst_hbm,
    counts_hbm,
    inv_hbm,
    agg_hbm,
    bundle_hbm,
    w_self_ref,
    w_neigh_ref,
    adj_ref,
    out_ref,
    self_ref,
    grads_ref,
    dst_ref,
    counts_ref,
    inv_ref,
    agg_ref,
    bundle_ref,
    out_all,
    scaled,
    adj,
    sems,
    small,
):
    hidden, slab = agg_ref.shape
    rows = w_self_ref.shape[0]
    tiles = grads_ref.shape[0]
    chunk = chunk_of(tiles)
    step_rows = chunk * BLK
    copies = [
        pltpu.make_async_copy(source, target, small.at[i])
        for i, (source, target) in enumerate(
            (
                (bundle_hbm, bundle_ref),
                (agg_hbm, agg_ref),
                (inv_hbm, inv_ref),
                (dst_hbm, dst_ref),
                (counts_hbm, counts_ref),
            )
        )
    ]
    for copy in copies + tile_copies(adj_ref, adj, sems, step_rows):
        copy.start()
    for copy in copies:
        copy.wait()
    weights = 2 * slab
    tail = bundle_ref[:, weights + 2 * hidden : weights + 2 * hidden + BLK].astype(f32)
    bias = tail[:, 0:1] + tail[:, 1:2] + tail[:, 2:3]
    w_self_all = bundle_ref[:, weights : weights + hidden]
    w_neigh_all = bundle_ref[:, weights + hidden : weights + 2 * hidden]
    contract_rows = (((0,), (0,)), ((), ()))
    width = 2 * BLK
    for start in range(0, slab, width):
        columns = slice(start, start + width)
        preact = (
            lax.dot_general(
                w_self_all, bundle_ref[:, columns], contract_rows, preferred_element_type=f32
            )
            + lax.dot_general(
                w_neigh_all, agg_ref[:, columns], contract_rows, preferred_element_type=f32
            )
            + bias
        )
        s = 1.0 / (1.0 + jnp.exp(-preact))
        silu = preact * s
        out_all[:, columns] = silu.astype(bf16)
        cotangent = bundle_ref[:, slab + start : slab + start + width].astype(f32)
        d_preact = (cotangent * (s + silu * (1.0 - s))).astype(bf16)
        self_ref[:, columns] = jnp.dot(w_self_ref[...], d_preact, preferred_element_type=f32)
        neigh = jnp.dot(w_neigh_ref[...], d_preact, preferred_element_type=f32)
        for half in range(width // BLK):
            n = start // BLK + half
            part = neigh[:, half * BLK : (half + 1) * BLK] * inv_ref[n : n + 1]
            scaled[n] = part.astype(bf16)
    first = pl.multiple_of(lax.axis_index("feat") * rows, rows)
    out_ref[...] = out_all[pl.ds(first, rows), :]

    zero = jnp.zeros((rows, BLK), bf16)
    contract_columns = (((1,), (1,)), ((), ()))

    def step(k, carry):
        wait_tiles(adj_ref, adj, sems, step_rows, k)
        for i in range(chunk):
            t = k * chunk + i
            q = k * (chunk // CAP) + i // CAP
            live = (i % CAP) < counts_ref[0, q]
            chosen = jnp.where(live, scaled[dst_ref[i % CAP, q]], zero)
            start = pl.multiple_of(t * BLK, BLK)
            grads = lax.dot_general(
                chosen, adj[pl.ds(start, BLK), :], contract_columns, preferred_element_type=f32
            )
            grads_ref[t] = grads.astype(bf16)
        return carry

    lax.fori_loop(0, tiles // chunk, step, 0)


def sum_kernel(ids_ref, grads_ref, self_ref, out_ref):
    tiles = grads_ref.shape[0]
    along = ids_ref.shape[0]
    column = tiles // (along * CAP)

    def step(q, sums):
        for c in range(CAP):
            block = grads_ref[q * CAP + c].astype(f32)
            asked = ids_ref[q // column, c, q % column]
            sums = [total + jnp.where(asked == n, block, 0.0) for n, total in enumerate(sums)]
        return tuple(sums)

    start = tuple(self_ref[:, n * BLK : (n + 1) * BLK] for n in range(NB))
    sums = lax.fori_loop(0, tiles // CAP, step, start, unroll=2)
    for n in range(NB):
        out_ref[:, n * BLK : (n + 1) * BLK] = sums[n]


def params(limit=VMEM_LIMIT):
    return pltpu.CompilerParams(vmem_limit_bytes=limit)


def shape(dims, dtype):
    return jax.ShapeDtypeStruct(dims, dtype)


def per_device(feats, w_self, w_neigh, bias, cotangent, block_ids, req_counts, tile_dst, adjacency):
    along, column = lax.axis_size("x"), lax.axis_size("z")
    graph_parts = along * column
    hidden = w_self.shape[1]
    rows, slab = feats.shape
    tiles = graph_parts * CAP
    per_row = column * CAP
    adj = adjacency.reshape(tiles * BLK, BLK)
    dst = tile_dst[0].T
    width = 2 * slab + 2 * hidden + BLK

    packed, ask, bundle = pl.pallas_call(
        prepare_kernel,
        out_shape=(
            shape((rows, slab + CAP * BLK), bf16),
            shape((along, CAP, BLK), jnp.int32),
            shape((rows, width), bf16),
        ),
        in_specs=[HBM] * 6,
        out_specs=(VMEM,) * 3,
        scratch_shapes=[
            pltpu.VMEM((8, BLK), jnp.int32),
            pltpu.VMEM((CAP, graph_parts), jnp.int32),
            pltpu.VMEM((1, rows), f32),
            pltpu.SemaphoreType.DMA((7,)),
        ],
        compiler_params=params(66_800_000),
        name="prepare",
    )(block_ids[0].T, bias.reshape(1, rows), feats, cotangent, w_self, w_neigh)
    bundle = lax.all_gather(bundle, "feat", axis=0, tiled=True)
    asked = lax.all_to_all(ask, "x", 0, 0)
    slabs = lax.all_gather(packed, "z", axis=0)
    picked = pl.pallas_call(
        select_kernel,
        out_shape=shape((along, per_row + CAP, rows, BLK), bf16),
        in_specs=[SMEM, VMEM],
        out_specs=VMEM,
        compiler_params=params(),
        name="select_blocks",
    )(asked, slabs)
    fetched = lax.all_to_all(picked, "x", 0, 0)
    steps = along * per_row // chunk_of(per_row)
    agg, inverse = pl.pallas_call(
        aggregate_kernel,
        out_shape=(shape((rows, slab), bf16), shape((NB, BLK), f32)),
        in_specs=[HBM, HBM, VMEM, HBM],
        out_specs=(VMEM, HBM),
        scratch_shapes=[
            pltpu.SMEM((CAP, graph_parts), jnp.int32),
            pltpu.SMEM((1, graph_parts), jnp.int32),
            pltpu.VMEM((NB, BLK), f32),
            pltpu.VMEM((tiles * BLK, BLK), bf16),
            pltpu.SemaphoreType.DMA((steps,)),
            pltpu.SemaphoreType.DMA((3,)),
        ],
        compiler_params=params(66_400_000),
        name="aggregate",
    )(dst, req_counts, fetched, adj)
    agg_all = lax.all_gather(agg, "feat", axis=0, tiled=True)
    output, self_grad, grads = pl.pallas_call(
        update_kernel,
        out_shape=(
            shape((rows, slab), bf16),
            shape((rows, slab), f32),
            shape((tiles, rows, BLK), bf16),
        ),
        in_specs=[HBM] * 5 + [VMEM] * 2 + [HBM],
        out_specs=(VMEM,) * 3,
        scratch_shapes=[
            pltpu.SMEM((CAP, graph_parts), jnp.int32),
            pltpu.SMEM((1, graph_parts), jnp.int32),
            pltpu.VMEM((NB, BLK), f32),
            pltpu.VMEM((hidden, slab), bf16),
            pltpu.VMEM((hidden, width), bf16),
            pltpu.VMEM((hidden, slab), bf16),
            pltpu.VMEM((NB, rows, BLK), bf16),
            pltpu.VMEM((tiles * BLK, BLK), bf16),
            pltpu.SemaphoreType.DMA((tiles // chunk_of(tiles),)),
            pltpu.SemaphoreType.DMA((5,)),
        ],
        compiler_params=params(66_800_000),
        name="update",
    )(dst, req_counts, inverse, agg_all, bundle, w_self, w_neigh, adj)
    returned = lax.all_to_all(
        grads.reshape(graph_parts, CAP, rows, BLK), ("x", "z"), 0, 0
    ).reshape(tiles, rows, BLK)
    me = lax.axis_index("x") * column + lax.axis_index("z")
    ids = lax.dynamic_slice(
        fetched, (0, per_row, 0, me), (along, CAP, rows, 1)
    )
    ids = ids.reshape(along, CAP, rows).astype(jnp.int32)
    feat_grad = pl.pallas_call(
        sum_kernel,
        out_shape=shape((rows, slab), f32),
        in_specs=[SMEM, VMEM, VMEM],
        out_specs=VMEM,
        compiler_params=params(),
        name="sum_returned",
    )(ids, returned, self_grad)
    return (output, feat_grad)


def solution(mesh):
    graph, feat = mesh.devices.shape
    along = 4 if graph % 12 == 0 else 2
    mesh = Mesh(mesh.devices.reshape(along, graph // along, feat), ("x", "z", "feat"))
    graph = ("x", "z")
    in_specs = (
        P("feat", graph),
        P("feat", None),
        P("feat", None),
        P("feat"),
        P("feat", graph),
        P(graph, None, None),
        P(graph, None),
        P(graph, None, None),
        P(graph, None, None, None, None),
    )
    out_specs = (P("feat", graph), P("feat", graph))
    return jax.shard_map(
        per_device, mesh=mesh, in_specs=in_specs, out_specs=out_specs, check_vma=False
    )
```

```python
import jax
import jax.numpy as jnp
from jax import lax
from jax.experimental import pallas as pl
from jax.experimental.pallas import tpu as pltpu
from jax.sharding import Mesh, PartitionSpec as P

BLK = 128
NB = 8
CAP = 2
VMEM_LIMIT = 24 * 1024 * 1024

SMEM = pl.BlockSpec(memory_space=pltpu.SMEM)
VMEM = pl.BlockSpec(memory_space=pltpu.VMEM)
HBM = pl.BlockSpec(memory_space=pltpu.HBM)

f32 = jnp.float32
bf16 = jnp.bfloat16


def chunk_of(tiles):
    return 8 if tiles % 8 == 0 else tiles


def prepare_kernel(
    ids_hbm,
    bias_hbm,
    feats_hbm,
    cot_hbm,
    w_self_hbm,
    w_neigh_hbm,
    slab_ref,
    ask_ref,
    out_hbm,
    bundle_ref,
    pad,
    ids_ref,
    bias_ref,
    sems,
    out_sems,
):
    rows, slab = feats_hbm.shape
    parts = ids_hbm.shape[1]
    hidden = w_self_hbm.shape[1]
    ends = (0, slab, 2 * slab, 2 * slab + hidden, 2 * slab + 2 * hidden)
    pieces = [bundle_ref.at[:, pl.ds(i, j - i)] for i, j in zip(ends, ends[1:])]
    sources = (ids_hbm, bias_hbm, feats_hbm, feats_hbm, cot_hbm, w_self_hbm, w_neigh_hbm)
    targets = [ids_ref, bias_ref, slab_ref.at[:, pl.ds(0, slab)]] + pieces
    copies = [
        pltpu.make_async_copy(source, target, sems.at[i])
        for i, (source, target) in enumerate(zip(sources, targets))
    ]
    for copy in copies:
        copy.start()
    pad[...] = jnp.zeros_like(pad)
    copies[0].wait()
    pad[0:CAP, 0:parts] = ids_ref[...]
    ask_ref[...] = pad[0:CAP, :]
    row = lax.broadcasted_iota(jnp.int32, (rows, BLK), 0)
    mine = row == lax.axis_index("z")
    for c in range(CAP):
        ids = jnp.broadcast_to(pad[c : c + 1, :], (rows, BLK))
        plane = jnp.where(mine, ids, 0).astype(f32).astype(bf16)
        slab_ref[:, slab + c * BLK : slab + (c + 1) * BLK] = plane
    copies[1].wait()
    wide = jnp.broadcast_to(bias_ref[...], (rows, rows))
    place = lax.broadcasted_iota(jnp.int32, (rows, rows), 0)
    place = place == lax.broadcasted_iota(jnp.int32, (rows, rows), 1)
    bias = jnp.sum(jnp.where(place, wide, 0.0), axis=1, keepdims=True)
    high = bias.astype(bf16).astype(f32)
    middle = (bias - high).astype(bf16).astype(f32)
    low = bias - high - middle
    lane = lax.broadcasted_iota(jnp.int32, (rows, BLK), 1)
    terms = jnp.where(lane == 0, high, jnp.where(lane == 1, middle, jnp.where(lane == 2, low, 0.0)))
    bundle_ref[:, ends[-1] :] = terms.astype(bf16)
    for copy in copies[2:]:
        copy.wait()
    copies = [
        pltpu.make_async_copy(bundle_ref, out_hbm.at[i], out_sems.at[i])
        for i in range(out_hbm.shape[0])
    ]
    for copy in copies:
        copy.start()
    for copy in copies:
        copy.wait()


def select_kernel(*refs):
    *asks, slabs_ref, out_ref, ask_ref, sems = refs
    copies = [
        pltpu.make_async_copy(ask, ask_ref.at[s], sems.at[s]) for s, ask in enumerate(asks)
    ]
    for copy in copies:
        copy.start()
    along, _, rows, _ = out_ref.shape
    column = slabs_ref.shape[0]
    slab = NB * BLK
    x = lax.axis_index("x")
    for c in range(CAP):
        plane = jnp.zeros((rows, BLK), f32)
        for k in range(column):
            plane += slabs_ref[k, :, slab + c * BLK : slab + (c + 1) * BLK].astype(f32)
        for i in range(along):
            out_ref[i, column * CAP + c] = plane.astype(bf16)
    for s in range(along):
        copies[s].wait()
        i = lax.rem(x - s + along, along)
        for k in range(column):
            for c in range(CAP):
                start = pl.multiple_of(ask_ref[s, c, x * column + k] * BLK, BLK)
                out_ref[i, k * CAP + c] = slabs_ref[k, :, pl.ds(start, BLK)]


def tile_copies(adj_ref, adj, sems, step):
    return [
        pltpu.make_async_copy(
            adj_ref.at[pl.ds(k * step, step)], adj.at[pl.ds(k * step, step)], sems.at[k]
        )
        for k in range(adj_ref.shape[0] // step)
    ]


def wait_tiles(adj_ref, adj, sems, step, k):
    part = pl.ds(pl.multiple_of(k * step, step), step)
    pltpu.make_async_copy(adj_ref.at[part], adj.at[part], sems.at[k]).wait()


def aggregate_kernel(
    dst_hbm, counts_hbm, fetched_ref, adj_ref, agg_ref, inv_hbm, dst_ref, counts_ref, inv, adj, sems, small
):
    along, slots, rows, _ = fetched_ref.shape
    per_row = slots - CAP
    chunk = chunk_of(per_row)
    step_rows = chunk * BLK
    dst_copy = pltpu.make_async_copy(dst_hbm, dst_ref, small.at[0])
    counts_copy = pltpu.make_async_copy(counts_hbm, counts_ref, small.at[1])
    dst_copy.start()
    counts_copy.start()
    for copy in tile_copies(adj_ref, adj, sems, step_rows):
        copy.start()
    row_ids = lax.broadcasted_iota(jnp.int32, (16, BLK), 0)
    zero = jnp.zeros((rows, BLK), bf16)
    chunks = per_row // chunk
    dst_copy.wait()
    counts_copy.wait()

    def step(k, acc):
        columns = []
        for i in range(chunk):
            q = k * (chunk // CAP) + i // CAP
            live = (i % CAP) < counts_ref[0, q]
            dst = jnp.where(live, dst_ref[i % CAP, q], NB)
            block = fetched_ref[k // chunks, (k % chunks) * chunk + i]
            pieces = [jnp.where(dst == n, block, zero) for n in range(NB)]
            pieces.append((row_ids == dst).astype(f32).astype(bf16))
            columns.append(jnp.concatenate(pieces, axis=0))
        lhs = jnp.concatenate(columns, axis=1)
        wait_tiles(adj_ref, adj, sems, step_rows, k)
        weights = adj[pl.ds(pl.multiple_of(k * step_rows, step_rows), step_rows), :]
        return acc + jnp.dot(lhs, weights, preferred_element_type=f32)

    acc = lax.fori_loop(0, along * chunks, step, jnp.zeros((NB * rows + 16, BLK), f32))
    inverse = 1.0 / jnp.maximum(acc[NB * rows : NB * rows + NB], 1.0)
    inv[...] = inverse
    inv_copy = pltpu.make_async_copy(inv, inv_hbm, small.at[2])
    inv_copy.start()
    for n in range(NB):
        part = acc[n * rows : (n + 1) * rows] * inverse[n : n + 1]
        agg_ref[:, n * BLK : (n + 1) * BLK] = part.astype(bf16)
    inv_copy.wait()


def update_kernel(
    dst_hbm,
    counts_hbm,
    inv_hbm,
    agg_hbm,
    bundle_hbm,
    w_self_ref,
    w_neigh_ref,
    adj_ref,
    out_ref,
    self_ref,
    grads_ref,
    dst_ref,
    counts_ref,
    inv_ref,
    agg_ref,
    bundle_ref,
    out_all,
    scaled,
    adj,
    sems,
    small,
):
    hidden, slab = agg_ref.shape
    rows = w_self_ref.shape[0]
    tiles = grads_ref.shape[0]
    chunk = chunk_of(tiles)
    step_rows = chunk * BLK
    copies = [
        pltpu.make_async_copy(source, target, small.at[i])
        for i, (source, target) in enumerate(
            (
                (bundle_hbm, bundle_ref),
                (agg_hbm, agg_ref),
                (inv_hbm, inv_ref),
                (dst_hbm, dst_ref),
                (counts_hbm, counts_ref),
            )
        )
    ]
    for copy in copies + tile_copies(adj_ref, adj, sems, step_rows):
        copy.start()
    for copy in copies:
        copy.wait()
    weights = 2 * slab
    tail = bundle_ref[:, weights + 2 * hidden : weights + 2 * hidden + BLK].astype(f32)
    bias = tail[:, 0:1] + tail[:, 1:2] + tail[:, 2:3]
    w_self_all = bundle_ref[:, weights : weights + hidden]
    w_neigh_all = bundle_ref[:, weights + hidden : weights + 2 * hidden]
    contract_rows = (((0,), (0,)), ((), ()))
    width = 2 * BLK
    for start in range(0, slab, width):
        columns = slice(start, start + width)
        preact = (
            lax.dot_general(
                w_self_all, bundle_ref[:, columns], contract_rows, preferred_element_type=f32
            )
            + lax.dot_general(
                w_neigh_all, agg_ref[:, columns], contract_rows, preferred_element_type=f32
            )
            + bias
        )
        s = 1.0 / (1.0 + jnp.exp(-preact))
        silu = preact * s
        out_all[:, columns] = silu.astype(bf16)
        cotangent = bundle_ref[:, slab + start : slab + start + width].astype(f32)
        d_preact = (cotangent * (s + silu * (1.0 - s))).astype(bf16)
        self_ref[:, columns] = jnp.dot(w_self_ref[...], d_preact, preferred_element_type=f32)
        neigh = jnp.dot(w_neigh_ref[...], d_preact, preferred_element_type=f32)
        for half in range(width // BLK):
            n = start // BLK + half
            part = neigh[:, half * BLK : (half + 1) * BLK] * inv_ref[n : n + 1]
            scaled[n] = part.astype(bf16)
    first = pl.multiple_of(lax.axis_index("feat") * rows, rows)
    out_ref[...] = out_all[pl.ds(first, rows), :]

    zero = jnp.zeros((rows, BLK), bf16)
    contract_columns = (((1,), (1,)), ((), ()))

    def step(k, carry):
        wait_tiles(adj_ref, adj, sems, step_rows, k)
        for i in range(chunk):
            t = k * chunk + i
            q = k * (chunk // CAP) + i // CAP
            live = (i % CAP) < counts_ref[0, q]
            chosen = jnp.where(live, scaled[dst_ref[i % CAP, q]], zero)
            start = pl.multiple_of(t * BLK, BLK)
            grads = lax.dot_general(
                chosen, adj[pl.ds(start, BLK), :], contract_columns, preferred_element_type=f32
            )
            grads_ref[t] = grads.astype(bf16)
        return carry

    lax.fori_loop(0, tiles // chunk, step, 0)


def sum_kernel(ids_ref, grads_ref, self_hbm, out_ref, self_ref, sem):
    self_copy = pltpu.make_async_copy(self_hbm, self_ref, sem)
    self_copy.start()
    tiles, rows, _ = grads_ref.shape
    along = ids_ref.shape[0]
    column = tiles // (along * CAP)

    def step(q, sums):
        for c in range(CAP):
            block = grads_ref[q * CAP + c].astype(f32)
            asked = ids_ref[q // column, c, q % column]
            sums = [total + jnp.where(asked == n, block, 0.0) for n, total in enumerate(sums)]
        return tuple(sums)

    start = (jnp.zeros((rows, BLK), f32),) * NB
    sums = lax.fori_loop(0, tiles // CAP, step, start, unroll=2)
    self_copy.wait()
    for n in range(NB):
        columns = slice(n * BLK, (n + 1) * BLK)
        out_ref[:, columns] = self_ref[:, columns] + sums[n]


def params(limit=VMEM_LIMIT):
    return pltpu.CompilerParams(vmem_limit_bytes=limit)


def shape(dims, dtype):
    return jax.ShapeDtypeStruct(dims, dtype)


def per_device(feats, w_self, w_neigh, bias, cotangent, block_ids, req_counts, tile_dst, adjacency):
    along, column = lax.axis_size("x"), lax.axis_size("z")
    graph_parts = along * column
    hidden = w_self.shape[1]
    rows, slab = feats.shape
    tiles = graph_parts * CAP
    per_row = column * CAP
    adj = adjacency.reshape(tiles * BLK, BLK)
    dst = tile_dst[0].T
    width = 2 * slab + 2 * hidden + BLK
    receivers = lax.axis_size("feat")

    packed, ask, bundle = pl.pallas_call(
        prepare_kernel,
        out_shape=(
            shape((rows, slab + CAP * BLK), bf16),
            shape((CAP, BLK), jnp.int32),
            shape((receivers, rows, width), bf16),
        ),
        in_specs=[HBM] * 6,
        out_specs=(VMEM, VMEM, HBM),
        scratch_shapes=[
            pltpu.VMEM((rows, width), bf16),
            pltpu.VMEM((8, BLK), jnp.int32),
            pltpu.VMEM((CAP, graph_parts), jnp.int32),
            pltpu.VMEM((1, rows), f32),
            pltpu.SemaphoreType.DMA((7,)),
            pltpu.SemaphoreType.DMA((receivers,)),
        ],
        compiler_params=params(66_800_000),
        name="prepare",
    )(block_ids[0].T, bias.reshape(1, rows), feats, cotangent, w_self, w_neigh)
    bundle = lax.all_to_all(bundle, "feat", 0, 0).reshape(hidden, width)
    asked = [ask] + [
        lax.ppermute(ask, "x", [(i, (i + s) % along) for i in range(along)])
        for s in range(1, along)
    ]
    slabs = lax.all_gather(packed, "z", axis=0)
    picked = pl.pallas_call(
        select_kernel,
        out_shape=shape((along, per_row + CAP, rows, BLK), bf16),
        in_specs=[HBM] * along + [VMEM],
        out_specs=VMEM,
        scratch_shapes=[
            pltpu.SMEM((along, CAP, BLK), jnp.int32),
            pltpu.SemaphoreType.DMA((along,)),
        ],
        compiler_params=params(),
        name="select_blocks",
    )(*asked, slabs)
    picked, bundle = lax.optimization_barrier((picked, bundle))
    fetched = lax.all_to_all(picked, "x", 0, 0)
    steps = along * per_row // chunk_of(per_row)
    agg, inverse = pl.pallas_call(
        aggregate_kernel,
        out_shape=(shape((rows, slab), bf16), shape((NB, BLK), f32)),
        in_specs=[HBM, HBM, VMEM, HBM],
        out_specs=(VMEM, HBM),
        scratch_shapes=[
            pltpu.SMEM((CAP, graph_parts), jnp.int32),
            pltpu.SMEM((1, graph_parts), jnp.int32),
            pltpu.VMEM((NB, BLK), f32),
            pltpu.VMEM((tiles * BLK, BLK), bf16),
            pltpu.SemaphoreType.DMA((steps,)),
            pltpu.SemaphoreType.DMA((3,)),
        ],
        compiler_params=params(66_400_000),
        name="aggregate",
    )(dst, req_counts, fetched, adj)
    agg_all = lax.all_gather(agg, "feat", axis=0, tiled=True)
    output, self_grad, grads = pl.pallas_call(
        update_kernel,
        out_shape=(
            shape((rows, slab), bf16),
            shape((rows, slab), f32),
            shape((tiles, rows, BLK), bf16),
        ),
        in_specs=[HBM] * 5 + [VMEM] * 2 + [HBM],
        out_specs=(VMEM,) * 3,
        scratch_shapes=[
            pltpu.SMEM((CAP, graph_parts), jnp.int32),
            pltpu.SMEM((1, graph_parts), jnp.int32),
            pltpu.VMEM((NB, BLK), f32),
            pltpu.VMEM((hidden, slab), bf16),
            pltpu.VMEM((hidden, width), bf16),
            pltpu.VMEM((hidden, slab), bf16),
            pltpu.VMEM((NB, rows, BLK), bf16),
            pltpu.VMEM((tiles * BLK, BLK), bf16),
            pltpu.SemaphoreType.DMA((tiles // chunk_of(tiles),)),
            pltpu.SemaphoreType.DMA((5,)),
        ],
        compiler_params=params(66_800_000),
        name="update",
    )(dst, req_counts, inverse, agg_all, bundle, w_self, w_neigh, adj)
    returned = lax.all_to_all(
        grads.reshape(graph_parts, CAP, rows, BLK), ("x", "z"), 0, 0
    ).reshape(tiles, rows, BLK)
    me = lax.axis_index("x") * column + lax.axis_index("z")
    ids = lax.dynamic_slice(
        fetched, (0, per_row, 0, me), (along, CAP, rows, 1)
    )
    ids = ids.reshape(along, CAP, rows).astype(jnp.int32)
    feat_grad = pl.pallas_call(
        sum_kernel,
        out_shape=shape((rows, slab), f32),
        in_specs=[SMEM, VMEM, HBM],
        out_specs=VMEM,
        scratch_shapes=[pltpu.VMEM((rows, slab), f32), pltpu.SemaphoreType.DMA],
        compiler_params=params(66_500_000),
        name="sum_returned",
    )(ids, returned, self_grad)
    return (output, feat_grad)


def solution(mesh):
    graph, feat = mesh.devices.shape
    along = 4 if graph % 12 == 0 else 2
    mesh = Mesh(mesh.devices.reshape(along, graph // along, feat), ("x", "z", "feat"))
    graph = ("x", "z")
    in_specs = (
        P("feat", graph),
        P("feat", None),
        P("feat", None),
        P("feat"),
        P("feat", graph),
        P(graph, None, None),
        P(graph, None),
        P(graph, None, None),
        P(graph, None, None, None, None),
    )
    out_specs = (P("feat", graph), P("feat", graph))
    return jax.shard_map(
        per_device, mesh=mesh, in_specs=in_specs, out_specs=out_specs, check_vma=False
    )
```

```python
import jax
import jax.numpy as jnp
from jax import lax
from jax.experimental import pallas as pl
from jax.experimental.pallas import tpu as pltpu
from jax.sharding import Mesh, PartitionSpec as P

BLK = 128
NB = 8
CAP = 2
VMEM_LIMIT = 24 * 1024 * 1024

SMEM = pl.BlockSpec(memory_space=pltpu.SMEM)
VMEM = pl.BlockSpec(memory_space=pltpu.VMEM)
HBM = pl.BlockSpec(memory_space=pltpu.HBM)

f32 = jnp.float32
bf16 = jnp.bfloat16


def chunk_of(tiles):
    return 8 if tiles % 8 == 0 else tiles


def prepare_kernel(
    ids_hbm,
    bias_hbm,
    feats_hbm,
    cot_hbm,
    w_self_hbm,
    w_neigh_hbm,
    slab_ref,
    ask_ref,
    out_hbm,
    bundle_ref,
    pad,
    ids_ref,
    bias_ref,
    sems,
    out_sems,
):
    rows, slab = feats_hbm.shape
    parts = ids_hbm.shape[1]
    hidden = w_self_hbm.shape[1]
    ends = (0, slab, 2 * slab, 2 * slab + hidden, 2 * slab + 2 * hidden)
    pieces = [bundle_ref.at[:, pl.ds(i, j - i)] for i, j in zip(ends, ends[1:])]
    sources = (ids_hbm, bias_hbm, feats_hbm, feats_hbm, cot_hbm, w_self_hbm, w_neigh_hbm)
    targets = [ids_ref, bias_ref, slab_ref.at[:, pl.ds(0, slab)]] + pieces
    copies = [
        pltpu.make_async_copy(source, target, sems.at[i])
        for i, (source, target) in enumerate(zip(sources, targets))
    ]
    for copy in copies:
        copy.start()
    pad[...] = jnp.zeros_like(pad)
    copies[0].wait()
    pad[0:CAP, 0:parts] = ids_ref[...]
    ask_ref[...] = pad[0:CAP, :]
    row = lax.broadcasted_iota(jnp.int32, (rows, BLK), 0)
    mine = row == lax.axis_index("z")
    for c in range(CAP):
        ids = jnp.broadcast_to(pad[c : c + 1, :], (rows, BLK))
        plane = jnp.where(mine, ids, 0).astype(f32).astype(bf16)
        slab_ref[:, slab + c * BLK : slab + (c + 1) * BLK] = plane
    copies[1].wait()
    wide = jnp.broadcast_to(bias_ref[...], (rows, rows))
    place = lax.broadcasted_iota(jnp.int32, (rows, rows), 0)
    place = place == lax.broadcasted_iota(jnp.int32, (rows, rows), 1)
    bias = jnp.sum(jnp.where(place, wide, 0.0), axis=1, keepdims=True)
    high = bias.astype(bf16).astype(f32)
    middle = (bias - high).astype(bf16).astype(f32)
    low = bias - high - middle
    lane = lax.broadcasted_iota(jnp.int32, (rows, BLK), 1)
    terms = jnp.where(lane == 0, high, jnp.where(lane == 1, middle, jnp.where(lane == 2, low, 0.0)))
    bundle_ref[:, ends[-1] :] = terms.astype(bf16)
    for copy in copies[2:]:
        copy.wait()
    copies = [
        pltpu.make_async_copy(bundle_ref, out_hbm.at[i], out_sems.at[i])
        for i in range(out_hbm.shape[0])
    ]
    for copy in copies:
        copy.start()
    for copy in copies:
        copy.wait()


def select_kernel(ask_ref, slabs_ref, out_ref):
    along, _, rows, _ = out_ref.shape
    column = slabs_ref.shape[0]
    slab = NB * BLK
    first = lax.axis_index("x") * column
    for i in range(along):
        for k in range(column):
            for c in range(CAP):
                start = pl.multiple_of(ask_ref[i, c, first + k] * BLK, BLK)
                out_ref[i, k * CAP + c] = slabs_ref[k, :, pl.ds(start, BLK)]
    for c in range(CAP):
        plane = jnp.zeros((rows, BLK), f32)
        for k in range(column):
            plane += slabs_ref[k, :, slab + c * BLK : slab + (c + 1) * BLK].astype(f32)
        for i in range(along):
            out_ref[i, column * CAP + c] = plane.astype(bf16)


def tile_copies(adj_ref, adj, sems, step):
    return [
        pltpu.make_async_copy(
            adj_ref.at[pl.ds(k * step, step)], adj.at[pl.ds(k * step, step)], sems.at[k]
        )
        for k in range(adj_ref.shape[0] // step)
    ]


def wait_tiles(adj_ref, adj, sems, step, k):
    part = pl.ds(pl.multiple_of(k * step, step), step)
    pltpu.make_async_copy(adj_ref.at[part], adj.at[part], sems.at[k]).wait()


def aggregate_kernel(
    dst_hbm,
    counts_hbm,
    fetched_hbm,
    adj_ref,
    agg_ref,
    inv_hbm,
    dst_ref,
    counts_ref,
    fetched_ref,
    inv,
    acc_ref,
    adj,
    sems,
    small,
):
    along, slots, rows, _ = fetched_ref.shape
    per_row = slots - CAP
    chunk = chunk_of(per_row)
    step_rows = chunk * BLK
    dst_copy = pltpu.make_async_copy(dst_hbm, dst_ref, small.at[0])
    counts_copy = pltpu.make_async_copy(counts_hbm, counts_ref, small.at[1])
    fetched_copy = pltpu.make_async_copy(fetched_hbm, fetched_ref, small.at[3])
    fetched_copy.start()
    dst_copy.start()
    counts_copy.start()
    for copy in tile_copies(adj_ref, adj, sems, step_rows):
        copy.start()
    row_ids = lax.broadcasted_iota(jnp.int32, (16, BLK), 0)
    zero = jnp.zeros((rows, BLK), bf16)
    chunks = per_row // chunk
    dst_copy.wait()
    counts_copy.wait()
    fetched_copy.wait()

    acc_ref[...] = jnp.zeros_like(acc_ref)
    ones = jnp.ones((rows, BLK), bf16)

    def step(k, carry):
        wait_tiles(adj_ref, adj, sems, step_rows, k)
        products = []
        for i in range(chunk):
            block = fetched_ref[k // chunks, (k % chunks) * chunk + i]
            start = pl.multiple_of((k * chunk + i) * BLK, BLK)
            products.append(jnp.dot(jnp.concatenate([block, ones], axis=0), adj[pl.ds(start, BLK), :], preferred_element_type=f32))
        for i in range(chunk):
            q = k * (chunk // CAP) + i // CAP
            live = (i % CAP) < counts_ref[0, q]
            dst = jnp.where(live, dst_ref[i % CAP, q], NB)
            acc_ref[dst] += products[i][0 : rows + 8]
        return carry

    lax.fori_loop(0, along * chunks, step, 0)
    for n in range(NB):
        inv[n : n + 1] = 1.0 / jnp.maximum(acc_ref[n, rows : rows + 1], 1.0)
    inv_copy = pltpu.make_async_copy(inv, inv_hbm, small.at[2])
    inv_copy.start()
    for n in range(NB):
        part = acc_ref[n, 0:rows] * inv[n : n + 1]
        agg_ref[:, n * BLK : (n + 1) * BLK] = part.astype(bf16)
    inv_copy.wait()


def update_kernel(
    dst_hbm,
    counts_hbm,
    inv_hbm,
    agg_hbm,
    bundle_hbm,
    adj_ref,
    out_ref,
    self_ref,
    grads_ref,
    dst_ref,
    counts_ref,
    inv_ref,
    agg_ref,
    bundle_ref,
    out_all,
    scaled,
    adj,
    sems,
    small,
):
    hidden, slab = agg_ref.shape
    tiles, rows, _ = grads_ref.shape
    chunk = chunk_of(tiles)
    step_rows = chunk * BLK
    copies = [
        pltpu.make_async_copy(source, target, small.at[i])
        for i, (source, target) in enumerate(
            (
                (bundle_hbm, bundle_ref),
                (agg_hbm, agg_ref),
                (inv_hbm, inv_ref),
                (dst_hbm, dst_ref),
                (counts_hbm, counts_ref),
            )
        )
    ]
    for copy in copies:
        copy.start()
    for copy in copies:
        copy.wait()
    for copy in tile_copies(adj_ref, adj, sems, step_rows):
        copy.start()
    weights = 2 * slab
    first = pl.multiple_of(lax.axis_index("feat") * rows, rows)
    w_self = bundle_ref[pl.ds(first, rows), weights : weights + hidden]
    w_neigh = bundle_ref[pl.ds(first, rows), weights + hidden : weights + 2 * hidden]
    tail = bundle_ref[:, weights + 2 * hidden : weights + 2 * hidden + BLK].astype(f32)
    bias = tail[:, 0:1] + tail[:, 1:2] + tail[:, 2:3]
    w_self_all = bundle_ref[:, weights : weights + hidden]
    w_neigh_all = bundle_ref[:, weights + hidden : weights + 2 * hidden]
    contract_rows = (((0,), (0,)), ((), ()))
    width = 2 * BLK
    for start in range(0, slab, width):
        columns = slice(start, start + width)
        preact = (
            lax.dot_general(
                w_self_all, bundle_ref[:, columns], contract_rows, preferred_element_type=f32
            )
            + lax.dot_general(
                w_neigh_all, agg_ref[:, columns], contract_rows, preferred_element_type=f32
            )
            + bias
        )
        s = 1.0 / (1.0 + jnp.exp(-preact))
        silu = preact * s
        out_all[:, columns] = silu.astype(bf16)
        cotangent = bundle_ref[:, slab + start : slab + start + width].astype(f32)
        d_preact = (cotangent * (s + silu * (1.0 - s))).astype(bf16)
        self_ref[:, columns] = jnp.dot(w_self, d_preact, preferred_element_type=f32)
        neigh = jnp.dot(w_neigh, d_preact, preferred_element_type=f32)
        for half in range(width // BLK):
            n = start // BLK + half
            part = neigh[:, half * BLK : (half + 1) * BLK] * inv_ref[n : n + 1]
            scaled[n] = part.astype(bf16)
    out_ref[...] = out_all[pl.ds(first, rows), :]

    zero = jnp.zeros((rows, BLK), bf16)
    contract_columns = (((1,), (1,)), ((), ()))

    def step(k, carry):
        wait_tiles(adj_ref, adj, sems, step_rows, k)
        for i in range(chunk):
            t = k * chunk + i
            q = k * (chunk // CAP) + i // CAP
            live = (i % CAP) < counts_ref[0, q]
            chosen = jnp.where(live, scaled[dst_ref[i % CAP, q]], zero)
            start = pl.multiple_of(t * BLK, BLK)
            grads = lax.dot_general(
                chosen, adj[pl.ds(start, BLK), :], contract_columns, preferred_element_type=f32
            )
            grads_ref[t] = grads.astype(bf16)
        return carry

    lax.fori_loop(0, tiles // chunk, step, 0)


def sum_kernel(ids_ref, grads_ref, self_hbm, out_ref, self_ref, sums, sem):
    self_copy = pltpu.make_async_copy(self_hbm, self_ref, sem)
    self_copy.start()
    tiles, rows, _ = grads_ref.shape
    along = ids_ref.shape[0]
    column = tiles // (along * CAP)
    sums[...] = jnp.zeros_like(sums)
    for q in range(tiles // CAP):
        for c in range(CAP):
            block = grads_ref[q * CAP + c].astype(f32)
            sums[c, ids_ref[q // column, c, q % column]] += block
    self_copy.wait()
    for n in range(NB):
        columns = slice(n * BLK, (n + 1) * BLK)
        total = self_ref[:, columns]
        for c in range(CAP):
            total += sums[c, n]
        out_ref[:, columns] = total


def params(limit=VMEM_LIMIT):
    return pltpu.CompilerParams(vmem_limit_bytes=limit)


def shape(dims, dtype):
    return jax.ShapeDtypeStruct(dims, dtype)


def prepare(block_ids, bias, feats, cotangent, w_self, w_neigh, receivers):
    rows, slab = feats.shape
    hidden = w_self.shape[1]
    graph_parts = block_ids.shape[1]
    width = 2 * slab + 2 * hidden + BLK
    return pl.pallas_call(
        prepare_kernel,
        out_shape=(
            shape((rows, slab + CAP * BLK), bf16),
            shape((CAP, BLK), jnp.int32),
            shape((receivers, rows, width), bf16),
        ),
        in_specs=[HBM] * 6,
        out_specs=(VMEM, VMEM, HBM),
        scratch_shapes=[
            pltpu.VMEM((rows, width), bf16),
            pltpu.VMEM((8, BLK), jnp.int32),
            pltpu.VMEM((CAP, graph_parts), jnp.int32),
            pltpu.VMEM((1, rows), f32),
            pltpu.SemaphoreType.DMA((7,)),
            pltpu.SemaphoreType.DMA((receivers,)),
        ],
        compiler_params=params(66_800_000),
        name="prepare",
    )(block_ids, bias, feats, cotangent, w_self, w_neigh)


def select(asked, slabs, along):
    column, rows, _ = slabs.shape
    return pl.pallas_call(
        select_kernel,
        out_shape=shape((along, column * CAP + CAP, rows, BLK), bf16),
        in_specs=[SMEM, VMEM],
        out_specs=VMEM,
        compiler_params=params(),
        name="select_blocks",
    )(asked, slabs)


def aggregate(dst, counts, fetched, adj):
    along, slots, rows, _ = fetched.shape
    tiles = along * (slots - CAP)
    steps = tiles // chunk_of(slots - CAP)
    return pl.pallas_call(
        aggregate_kernel,
        out_shape=(shape((rows, NB * BLK), bf16), shape((NB, BLK), f32)),
        in_specs=[HBM] * 4,
        out_specs=(VMEM, HBM),
        scratch_shapes=[
            pltpu.SMEM(dst.shape, jnp.int32),
            pltpu.SMEM(counts.shape, jnp.int32),
            pltpu.VMEM(fetched.shape, bf16),
            pltpu.VMEM((NB, BLK), f32),
            pltpu.VMEM((NB + 1, rows + 8, BLK), f32),
            pltpu.VMEM((tiles * BLK, BLK), bf16),
            pltpu.SemaphoreType.DMA((steps,)),
            pltpu.SemaphoreType.DMA((4,)),
        ],
        compiler_params=params(66_400_000),
        name="aggregate",
    )(dst, counts, fetched, adj)


def update(dst, counts, inverse, agg, bundle, adj, rows):
    hidden, slab = agg.shape
    tiles = adj.shape[0] // BLK
    return pl.pallas_call(
        update_kernel,
        out_shape=(
            shape((rows, slab), bf16),
            shape((rows, slab), f32),
            shape((tiles, rows, BLK), bf16),
        ),
        in_specs=[HBM] * 6,
        out_specs=(VMEM,) * 3,
        scratch_shapes=[
            pltpu.SMEM(dst.shape, jnp.int32),
            pltpu.SMEM(counts.shape, jnp.int32),
            pltpu.VMEM((NB, BLK), f32),
            pltpu.VMEM((hidden, slab), bf16),
            pltpu.VMEM(bundle.shape, bf16),
            pltpu.VMEM((hidden, slab), bf16),
            pltpu.VMEM((NB, rows, BLK), bf16),
            pltpu.VMEM((tiles * BLK, BLK), bf16),
            pltpu.SemaphoreType.DMA((tiles // chunk_of(tiles),)),
            pltpu.SemaphoreType.DMA((5,)),
        ],
        compiler_params=params(66_800_000),
        name="update",
    )(dst, counts, inverse, agg, bundle, adj)


def sum_returned(ids, returned, self_grad):
    return pl.pallas_call(
        sum_kernel,
        out_shape=shape(self_grad.shape, f32),
        in_specs=[SMEM, VMEM, HBM],
        out_specs=VMEM,
        scratch_shapes=[
            pltpu.VMEM(self_grad.shape, f32),
            pltpu.VMEM((CAP, NB, returned.shape[1], BLK), f32),
            pltpu.SemaphoreType.DMA,
        ],
        compiler_params=params(),
        name="sum_returned",
    )(ids, returned, self_grad)


def per_device(feats, w_self, w_neigh, bias, cotangent, block_ids, req_counts, tile_dst, adjacency):
    along, column = lax.axis_size("x"), lax.axis_size("z")
    graph_parts = along * column
    hidden = w_self.shape[1]
    rows, slab = feats.shape
    tiles = graph_parts * CAP
    per_row = column * CAP
    adj = adjacency.reshape(tiles * BLK, BLK)
    dst = tile_dst[0].T
    receivers = lax.axis_size("feat")

    packed, ask, bundle = prepare(
        block_ids[0].T, bias.reshape(1, rows), feats, cotangent, w_self, w_neigh, receivers
    )
    bundle = lax.all_to_all(bundle, "feat", 0, 0).reshape(hidden, -1)
    asked = lax.all_gather(ask, "x", axis=0)
    slabs = lax.all_gather(packed, "z", axis=0)
    picked = select(asked, slabs, along)
    picked, bundle = lax.optimization_barrier((picked, bundle))
    fetched = lax.all_to_all(picked, "x", 0, 0)
    agg, inverse = aggregate(dst, req_counts, fetched, adj)
    agg_all = lax.all_gather(agg, "feat", axis=0, tiled=True)
    output, self_grad, grads = update(
        dst, req_counts, inverse, agg_all, bundle, adj, rows
    )
    returned = lax.all_to_all(
        grads.reshape(graph_parts, CAP, rows, BLK), ("x", "z"), 0, 0
    ).reshape(tiles, rows, BLK)
    me = lax.axis_index("x") * column + lax.axis_index("z")
    ids = lax.dynamic_slice(fetched, (0, per_row, 0, me), (along, CAP, rows, 1))
    ids = ids.reshape(along, CAP, rows).astype(jnp.int32)
    feat_grad = sum_returned(ids, returned, self_grad)
    return (output, feat_grad)


def solution(mesh):
    graph, feat = mesh.devices.shape
    along = 4 if graph % 12 == 0 else 2
    mesh = Mesh(mesh.devices.reshape(along, graph // along, feat), ("x", "z", "feat"))
    graph = ("x", "z")
    in_specs = (
        P("feat", graph),
        P("feat", None),
        P("feat", None),
        P("feat"),
        P("feat", graph),
        P(graph, None, None),
        P(graph, None),
        P(graph, None, None),
        P(graph, None, None, None, None),
    )
    out_specs = (P("feat", graph), P("feat", graph))
    return jax.shard_map(
        per_device, mesh=mesh, in_specs=in_specs, out_specs=out_specs, check_vma=False
    )
```

```python
import jax
import jax.numpy as jnp
from jax import lax
from jax.experimental import pallas as pl
from jax.experimental.pallas import tpu as pltpu
from jax.sharding import Mesh, PartitionSpec as P

BLK = 128
NB = 8
CAP = 2
VMEM_LIMIT = 24 * 1024 * 1024

SMEM = pl.BlockSpec(memory_space=pltpu.SMEM)
VMEM = pl.BlockSpec(memory_space=pltpu.VMEM)
HBM = pl.BlockSpec(memory_space=pltpu.HBM)

f32 = jnp.float32
bf16 = jnp.bfloat16


def chunk_of(tiles):
    return 8 if tiles % 8 == 0 else tiles


def prepare_kernel(
    ids_hbm,
    bias_hbm,
    feats_hbm,
    cot_hbm,
    w_self_hbm,
    w_neigh_hbm,
    slabs_hbm,
    ask_ref,
    first_ref,
    second_ref,
    slab_ref,
    ids_ref,
    bias_ref,
    sems,
    out_sems,
):
    rows, slab = feats_hbm.shape
    parts = ids_hbm.shape[1]
    hidden = w_self_hbm.shape[1]
    left, right = pl.ds(0, slab), pl.ds(slab, hidden)
    copies = [
        pltpu.make_async_copy(source, target, sems.at[i])
        for i, (source, target) in enumerate(
            (
                (feats_hbm, slab_ref),
                (bias_hbm, bias_ref),
                (ids_hbm, ids_ref),
                (feats_hbm, first_ref.at[:, left]),
                (w_self_hbm, first_ref.at[:, right]),
                (cot_hbm, second_ref.at[:, left]),
                (w_neigh_hbm, second_ref.at[:, right]),
            )
        )
    ]
    for copy in copies:
        copy.start()
    copies[0].wait()
    out_copies = [
        pltpu.make_async_copy(slab_ref, slabs_hbm.at[i], out_sems.at[i])
        for i in range(slabs_hbm.shape[0])
    ]
    for copy in out_copies:
        copy.start()
    copies[1].wait()
    wide = jnp.broadcast_to(bias_ref[...], (rows, rows))
    place = lax.broadcasted_iota(jnp.int32, (rows, rows), 0)
    place = place == lax.broadcasted_iota(jnp.int32, (rows, rows), 1)
    bias = jnp.sum(jnp.where(place, wide, 0.0), axis=1, keepdims=True)
    high = bias.astype(bf16).astype(f32)
    middle = (bias - high).astype(bf16).astype(f32)
    low = bias - high - middle
    lane = lax.broadcasted_iota(jnp.int32, (rows, BLK), 1)
    terms = jnp.where(lane == 0, high, jnp.where(lane == 1, middle, jnp.where(lane == 2, low, 0.0)))
    second_ref[:, slab + hidden :] = terms.astype(bf16)
    copies[2].wait()
    ask_ref[...] = jnp.zeros_like(ask_ref)
    ask_ref[:, 0:parts] = ids_ref[...]
    for copy in copies[3:] + out_copies:
        copy.wait()


def tile_copies(adj_ref, adj, sems, step):
    return [
        pltpu.make_async_copy(
            adj_ref.at[pl.ds(k * step, step)], adj.at[pl.ds(k * step, step)], sems.at[k]
        )
        for k in range(adj_ref.shape[0] // step)
    ]


def wait_tiles(adj_ref, adj, sems, step, k):
    part = pl.ds(pl.multiple_of(k * step, step), step)
    pltpu.make_async_copy(adj_ref.at[part], adj.at[part], sems.at[k]).wait()


def aggregate_kernel(
    dst_hbm,
    counts_hbm,
    ids_hbm,
    slabs_hbm,
    adj_ref,
    agg_ref,
    inv_hbm,
    dst_ref,
    counts_ref,
    ids_ref,
    slabs_ref,
    inv,
    acc_ref,
    adj,
    sems,
    slab_sems,
    small,
):
    parts, rows, _ = slabs_ref.shape
    chunk = chunk_of(parts * CAP)
    step_rows = chunk * BLK
    step_parts = chunk // CAP
    small_copies = [
        pltpu.make_async_copy(source, target, small.at[i])
        for i, (source, target) in enumerate(
            ((dst_hbm, dst_ref), (counts_hbm, counts_ref), (ids_hbm, ids_ref))
        )
    ]
    for copy in small_copies:
        copy.start()
    for slab_copy, tile_copy in zip(
        tile_copies(slabs_hbm, slabs_ref, slab_sems, step_parts),
        tile_copies(adj_ref, adj, sems, step_rows),
    ):
        slab_copy.start()
        tile_copy.start()
    acc_ref[...] = jnp.zeros_like(acc_ref)
    ones = jnp.ones((rows, BLK), bf16)
    for copy in small_copies:
        copy.wait()

    def step(k, carry):
        wait_tiles(slabs_hbm, slabs_ref, slab_sems, step_parts, k)
        wait_tiles(adj_ref, adj, sems, step_rows, k)
        products = []
        for i in range(chunk):
            q = k * step_parts + i // CAP
            column = pl.multiple_of(ids_ref[i % CAP, q] * BLK, BLK)
            block = slabs_ref[q, :, pl.ds(column, BLK)]
            start = pl.multiple_of((k * chunk + i) * BLK, BLK)
            products.append(
                jnp.dot(
                    jnp.concatenate([block, ones], axis=0),
                    adj[pl.ds(start, BLK), :],
                    preferred_element_type=f32,
                )
            )
        for i in range(chunk):
            q = k * step_parts + i // CAP
            live = (i % CAP) < counts_ref[0, q]
            dst = jnp.where(live, dst_ref[i % CAP, q], NB)
            acc_ref[dst] += products[i][0 : rows + 8]
        return carry

    lax.fori_loop(0, parts * CAP // chunk, step, 0)
    for n in range(NB):
        inv[n : n + 1] = 1.0 / jnp.maximum(acc_ref[n, rows : rows + 1], 1.0)
    inv_copy = pltpu.make_async_copy(inv, inv_hbm, small.at[3])
    inv_copy.start()
    for n in range(NB):
        part = acc_ref[n, 0:rows] * inv[n : n + 1]
        agg_ref[:, n * BLK : (n + 1) * BLK] = part.astype(bf16)
    inv_copy.wait()


def update_kernel(
    dst_hbm,
    counts_hbm,
    inv_hbm,
    agg_hbm,
    first_hbm,
    second_hbm,
    adj_ref,
    out_ref,
    self_ref,
    grads_ref,
    dst_ref,
    counts_ref,
    inv_ref,
    agg_ref,
    first_ref,
    second_ref,
    out_all,
    scaled,
    adj,
    sems,
    small,
):
    hidden, slab = agg_ref.shape
    tiles, rows, _ = grads_ref.shape
    chunk = chunk_of(tiles)
    step_rows = chunk * BLK
    copies = [
        pltpu.make_async_copy(source, target, small.at[i])
        for i, (source, target) in enumerate(
            (
                (first_hbm, first_ref),
                (second_hbm, second_ref),
                (agg_hbm, agg_ref),
                (inv_hbm, inv_ref),
                (dst_hbm, dst_ref),
                (counts_hbm, counts_ref),
            )
        )
    ]
    for copy in copies:
        copy.start()
    for copy in copies:
        copy.wait()
    for copy in tile_copies(adj_ref, adj, sems, step_rows):
        copy.start()
    first = pl.multiple_of(lax.axis_index("feat") * rows, rows)
    w_self = first_ref[pl.ds(first, rows), slab:]
    w_neigh = second_ref[pl.ds(first, rows), slab : slab + hidden]
    tail = second_ref[:, slab + hidden :].astype(f32)
    bias = tail[:, 0:1] + tail[:, 1:2] + tail[:, 2:3]
    w_self_all = first_ref[:, slab:]
    w_neigh_all = second_ref[:, slab : slab + hidden]
    contract_rows = (((0,), (0,)), ((), ()))
    width = 2 * BLK
    for start in range(0, slab, width):
        columns = slice(start, start + width)
        preact = (
            lax.dot_general(
                w_self_all, first_ref[:, columns], contract_rows, preferred_element_type=f32
            )
            + lax.dot_general(
                w_neigh_all, agg_ref[:, columns], contract_rows, preferred_element_type=f32
            )
            + bias
        )
        s = 1.0 / (1.0 + jnp.exp(-preact))
        silu = preact * s
        out_all[:, columns] = silu.astype(bf16)
        cotangent = second_ref[:, columns].astype(f32)
        d_preact = (cotangent * (s + silu * (1.0 - s))).astype(bf16)
        self_ref[:, columns] = jnp.dot(w_self, d_preact, preferred_element_type=f32)
        neigh = jnp.dot(w_neigh, d_preact, preferred_element_type=f32)
        for half in range(width // BLK):
            n = start // BLK + half
            part = neigh[:, half * BLK : (half + 1) * BLK] * inv_ref[n : n + 1]
            scaled[n] = part.astype(bf16)
    out_ref[...] = out_all[pl.ds(first, rows), :]

    zero = jnp.zeros((rows, BLK), bf16)
    contract_columns = (((1,), (1,)), ((), ()))

    def step(k, carry):
        wait_tiles(adj_ref, adj, sems, step_rows, k)
        for i in range(chunk):
            t = k * chunk + i
            q = k * (chunk // CAP) + i // CAP
            live = (i % CAP) < counts_ref[0, q]
            chosen = jnp.where(live, scaled[dst_ref[i % CAP, q]], zero)
            start = pl.multiple_of(t * BLK, BLK)
            grads = lax.dot_general(
                chosen, adj[pl.ds(start, BLK), :], contract_columns, preferred_element_type=f32
            )
            grads_ref[t] = grads.astype(bf16)
        return carry

    lax.fori_loop(0, tiles // chunk, step, 0)


def sum_kernel(ids_ref, grads_ref, self_hbm, out_ref, self_ref, sums, sem):
    self_copy = pltpu.make_async_copy(self_hbm, self_ref, sem)
    self_copy.start()
    tiles, rows, _ = grads_ref.shape
    column = lax.axis_size("z")
    along = tiles // (column * CAP)
    me = lax.axis_index("x") * column + lax.axis_index("z")
    sums[...] = jnp.zeros_like(sums)
    for q in range(tiles // CAP):
        for c in range(CAP):
            block = grads_ref[q * CAP + c].astype(f32)
            row = ((q % column) * along + q // column) * CAP + c
            sums[c, ids_ref[row, me]] += block
    self_copy.wait()
    for n in range(NB):
        columns = slice(n * BLK, (n + 1) * BLK)
        total = self_ref[:, columns]
        for c in range(CAP):
            total += sums[c, n]
        out_ref[:, columns] = total


def params(limit=VMEM_LIMIT):
    return pltpu.CompilerParams(vmem_limit_bytes=limit)


def shape(dims, dtype):
    return jax.ShapeDtypeStruct(dims, dtype)


def prepare(block_ids, bias, feats, cotangent, w_self, w_neigh):
    rows, slab = feats.shape
    hidden = w_self.shape[1]
    parts = block_ids.shape[1]
    return pl.pallas_call(
        prepare_kernel,
        out_shape=(
            shape((parts, rows, slab), bf16),
            shape((CAP, BLK), jnp.int32),
            shape((rows, slab + hidden), bf16),
            shape((rows, slab + hidden + BLK), bf16),
        ),
        in_specs=[HBM] * 6,
        out_specs=(HBM, VMEM, VMEM, VMEM),
        scratch_shapes=[
            pltpu.VMEM((rows, slab), bf16),
            pltpu.VMEM((CAP, parts), jnp.int32),
            pltpu.VMEM((1, rows), f32),
            pltpu.SemaphoreType.DMA((7,)),
            pltpu.SemaphoreType.DMA((parts,)),
        ],
        compiler_params=params(66_800_000),
        name="prepare",
    )(block_ids, bias, feats, cotangent, w_self, w_neigh)


def aggregate(dst, counts, block_ids, slabs, adj):
    parts, rows, _ = slabs.shape
    tiles = parts * CAP
    steps = tiles // chunk_of(tiles)
    return pl.pallas_call(
        aggregate_kernel,
        out_shape=(shape((rows, NB * BLK), bf16), shape((NB, BLK), f32)),
        in_specs=[HBM] * 5,
        out_specs=(VMEM, HBM),
        scratch_shapes=[
            pltpu.SMEM(dst.shape, jnp.int32),
            pltpu.SMEM(counts.shape, jnp.int32),
            pltpu.SMEM(dst.shape, jnp.int32),
            pltpu.VMEM(slabs.shape, bf16),
            pltpu.VMEM((NB, BLK), f32),
            pltpu.VMEM((NB + 1, rows + 8, BLK), f32),
            pltpu.VMEM((tiles * BLK, BLK), bf16),
            pltpu.SemaphoreType.DMA((steps,)),
            pltpu.SemaphoreType.DMA((steps,)),
            pltpu.SemaphoreType.DMA((4,)),
        ],
        compiler_params=params(66_800_000),
        name="aggregate",
    )(dst, counts, block_ids, slabs, adj)


def update(dst, counts, inverse, agg, first, second, adj, rows):
    hidden, slab = agg.shape
    tiles = adj.shape[0] // BLK
    return pl.pallas_call(
        update_kernel,
        out_shape=(
            shape((rows, slab), bf16),
            shape((rows, slab), f32),
            shape((tiles, rows, BLK), bf16),
        ),
        in_specs=[HBM] * 7,
        out_specs=(VMEM,) * 3,
        scratch_shapes=[
            pltpu.SMEM(dst.shape, jnp.int32),
            pltpu.SMEM(counts.shape, jnp.int32),
            pltpu.VMEM((NB, BLK), f32),
            pltpu.VMEM((hidden, slab), bf16),
            pltpu.VMEM(first.shape, bf16),
            pltpu.VMEM(second.shape, bf16),
            pltpu.VMEM((hidden, slab), bf16),
            pltpu.VMEM((NB, rows, BLK), bf16),
            pltpu.VMEM((tiles * BLK, BLK), bf16),
            pltpu.SemaphoreType.DMA((tiles // chunk_of(tiles),)),
            pltpu.SemaphoreType.DMA((6,)),
        ],
        compiler_params=params(66_800_000),
        name="update",
    )(dst, counts, inverse, agg, first, second, adj)


def sum_returned(ids, returned, self_grad):
    return pl.pallas_call(
        sum_kernel,
        out_shape=shape(self_grad.shape, f32),
        in_specs=[SMEM, VMEM, HBM],
        out_specs=VMEM,
        scratch_shapes=[
            pltpu.VMEM(self_grad.shape, f32),
            pltpu.VMEM((CAP, NB, returned.shape[1], BLK), f32),
            pltpu.SemaphoreType.DMA,
        ],
        compiler_params=params(),
        name="sum_returned",
    )(ids, returned, self_grad)


def per_device(feats, w_self, w_neigh, bias, cotangent, block_ids, req_counts, tile_dst, adjacency):
    graph_parts = lax.axis_size("x") * lax.axis_size("z")
    rows, slab = feats.shape
    tiles = graph_parts * CAP
    adj = adjacency.reshape(tiles * BLK, BLK)
    dst = tile_dst[0].T
    own_ids = block_ids[0].T

    slabs, ask, first, second = prepare(
        own_ids, bias.reshape(1, rows), feats, cotangent, w_self, w_neigh
    )
    slabs = lax.all_to_all(slabs, ("x", "z"), 0, 0)
    first = lax.all_gather(first, "feat", axis=0, tiled=True)
    second = lax.all_gather(second, "feat", axis=0, tiled=True)
    slabs, first, second = lax.optimization_barrier((slabs, first, second))
    agg, inverse = aggregate(dst, req_counts, own_ids, slabs, adj)
    agg_all = lax.all_gather(agg, "feat", axis=0, tiled=True)
    output, self_grad, grads = update(
        dst, req_counts, inverse, agg_all, first, second, adj, rows
    )
    returned = lax.all_to_all(
        grads.reshape(graph_parts, CAP, rows, BLK), ("x", "z"), 0, 0
    ).reshape(tiles, rows, BLK)
    ids = lax.all_gather(ask, "x", axis=0, tiled=True)
    ids = lax.all_gather(ids, "z", axis=0, tiled=True)
    feat_grad = sum_returned(ids, returned, self_grad)
    return (output, feat_grad)


def solution(mesh):
    graph, feat = mesh.devices.shape
    along = 4 if graph % 12 == 0 else 2
    mesh = Mesh(mesh.devices.reshape(along, graph // along, feat), ("x", "z", "feat"))
    graph = ("x", "z")
    in_specs = (
        P("feat", graph),
        P("feat", None),
        P("feat", None),
        P("feat"),
        P("feat", graph),
        P(graph, None, None),
        P(graph, None),
        P(graph, None, None),
        P(graph, None, None, None, None),
    )
    out_specs = (P("feat", graph), P("feat", graph))
    return jax.shard_map(
        per_device, mesh=mesh, in_specs=in_specs, out_specs=out_specs, check_vma=False
    )
```

```python
import jax
import jax.numpy as jnp
from jax import lax
from jax.experimental import pallas as pl
from jax.experimental.pallas import tpu as pltpu
from jax.sharding import Mesh, PartitionSpec as P

BLK = 128
NB = 8
CAP = 2
VMEM_LIMIT = 24 * 1024 * 1024

SMEM = pl.BlockSpec(memory_space=pltpu.SMEM)
VMEM = pl.BlockSpec(memory_space=pltpu.VMEM)
HBM = pl.BlockSpec(memory_space=pltpu.HBM)

f32 = jnp.float32
bf16 = jnp.bfloat16


def chunk_of(tiles):
    return 48 if tiles % 48 == 0 else (24 if tiles % 24 == 0 else tiles)


def prepare_kernel(
    ids_hbm,
    bias_hbm,
    feats_hbm,
    cot_hbm,
    w_self_hbm,
    w_neigh_hbm,
    slab_ref,
    ask_ref,
    out_hbm,
    bundle_ref,
    pad,
    ids_ref,
    bias_ref,
    sems,
    out_sems,
):
    rows, slab = feats_hbm.shape
    parts = ids_hbm.shape[1]
    hidden = w_self_hbm.shape[1]
    ends = (0, slab, 2 * slab, 2 * slab + hidden, 2 * slab + 2 * hidden)
    pieces = [bundle_ref.at[:, pl.ds(i, j - i)] for i, j in zip(ends, ends[1:])]
    sources = (ids_hbm, bias_hbm, feats_hbm, feats_hbm, cot_hbm, w_self_hbm, w_neigh_hbm)
    targets = [ids_ref, bias_ref, slab_ref.at[:, pl.ds(0, slab)]] + pieces
    copies = [
        pltpu.make_async_copy(source, target, sems.at[i])
        for i, (source, target) in enumerate(zip(sources, targets))
    ]
    for copy in copies:
        copy.start()
    pad[...] = jnp.zeros_like(pad)
    copies[0].wait()
    pad[0:CAP, 0:parts] = ids_ref[...]
    ask_ref[...] = pad[0:CAP, :]
    row = lax.broadcasted_iota(jnp.int32, (rows, BLK), 0)
    mine = row == lax.axis_index("z")
    for c in range(CAP):
        ids = jnp.broadcast_to(pad[c : c + 1, :], (rows, BLK))
        plane = jnp.where(mine, ids, 0).astype(f32).astype(bf16)
        slab_ref[:, slab + c * BLK : slab + (c + 1) * BLK] = plane
    copies[1].wait()
    wide = jnp.broadcast_to(bias_ref[...], (rows, rows))
    place = lax.broadcasted_iota(jnp.int32, (rows, rows), 0)
    place = place == lax.broadcasted_iota(jnp.int32, (rows, rows), 1)
    bias = jnp.sum(jnp.where(place, wide, 0.0), axis=1, keepdims=True)
    high = bias.astype(bf16).astype(f32)
    middle = (bias - high).astype(bf16).astype(f32)
    low = bias - high - middle
    lane = lax.broadcasted_iota(jnp.int32, (rows, BLK), 1)
    terms = jnp.where(lane == 0, high, jnp.where(lane == 1, middle, jnp.where(lane == 2, low, 0.0)))
    bundle_ref[:, ends[-1] :] = terms.astype(bf16)
    for copy in copies[2:]:
        copy.wait()
    copies = [
        pltpu.make_async_copy(bundle_ref, out_hbm.at[i], out_sems.at[i])
        for i in range(out_hbm.shape[0])
    ]
    for copy in copies:
        copy.start()
    for copy in copies:
        copy.wait()


def select_kernel(ask_ref, slabs_ref, out_ref):
    along, _, rows, _ = out_ref.shape
    column = slabs_ref.shape[0]
    slab = NB * BLK
    first = lax.axis_index("x") * column
    for i in range(along):
        for k in range(column):
            for c in range(CAP):
                start = pl.multiple_of(ask_ref[i, c, first + k] * BLK, BLK)
                out_ref[i, k * CAP + c] = slabs_ref[k, :, pl.ds(start, BLK)]
    for c in range(CAP):
        plane = jnp.zeros((rows, BLK), f32)
        for k in range(column):
            plane += slabs_ref[k, :, slab + c * BLK : slab + (c + 1) * BLK].astype(f32)
        for i in range(along):
            out_ref[i, column * CAP + c] = plane.astype(bf16)


def aggregate_kernel(
    dst_hbm,
    counts_hbm,
    fetched_ref,
    adj_ref,
    agg_ref,
    inv_hbm,
    dst_ref,
    counts_ref,
    inv,
    acc_ref,
    small,
):
    along, slots, rows, _ = fetched_ref.shape
    per_row = slots - CAP
    chunk = chunk_of(per_row)
    dst_copy = pltpu.make_async_copy(dst_hbm, dst_ref, small.at[0])
    counts_copy = pltpu.make_async_copy(counts_hbm, counts_ref, small.at[1])
    dst_copy.start()
    counts_copy.start()
    row_ids = lax.broadcasted_iota(jnp.int32, (16, BLK), 0)
    zero = jnp.zeros((rows, BLK), bf16)
    chunks = per_row // chunk
    dst_copy.wait()
    counts_copy.wait()

    acc_ref[...] = jnp.zeros_like(acc_ref)
    ones = jnp.ones((rows, BLK), bf16)

    def step(k, carry):
        products = []
        for i in range(chunk):
            block = fetched_ref[k // chunks, (k % chunks) * chunk + i]
            start = pl.multiple_of((k * chunk + i) * BLK, BLK)
            products.append(jnp.dot(jnp.concatenate([block, ones], axis=0), adj_ref[pl.ds(start, BLK), :], preferred_element_type=f32))
        for i in range(chunk):
            q = k * (chunk // CAP) + i // CAP
            live = (i % CAP) < counts_ref[0, q]
            dst = jnp.where(live, dst_ref[i % CAP, q], NB)
            acc_ref[dst] += products[i][0 : rows + 8]
        return carry

    lax.fori_loop(0, along * chunks, step, 0)
    for n in range(NB):
        inv[n : n + 1] = 1.0 / jnp.maximum(acc_ref[n, rows : rows + 1], 1.0)
    inv_copy = pltpu.make_async_copy(inv, inv_hbm, small.at[2])
    inv_copy.start()
    for n in range(NB):
        part = acc_ref[n, 0:rows] * inv[n : n + 1]
        agg_ref[:, n * BLK : (n + 1) * BLK] = part.astype(bf16)
    inv_copy.wait()


def update_kernel(
    dst_hbm,
    counts_hbm,
    inv_hbm,
    agg_ref,
    bundle_hbm,
    adj_ref,
    out_ref,
    self_ref,
    grads_ref,
    dst_ref,
    counts_ref,
    inv_ref,
    bundle_ref,
    out_all,
    scaled,
    small,
):
    hidden, slab = agg_ref.shape
    tiles, rows, _ = grads_ref.shape
    chunk = chunk_of(tiles)
    copies = [
        pltpu.make_async_copy(source, target, small.at[i])
        for i, (source, target) in enumerate(
            (
                (bundle_hbm, bundle_ref),
                (inv_hbm, inv_ref),
                (dst_hbm, dst_ref),
                (counts_hbm, counts_ref),
            )
        )
    ]
    for copy in copies:
        copy.start()
    for copy in copies:
        copy.wait()
    weights = 2 * slab
    first = pl.multiple_of(lax.axis_index("feat") * rows, rows)
    w_self = bundle_ref[pl.ds(first, rows), weights : weights + hidden]
    w_neigh = bundle_ref[pl.ds(first, rows), weights + hidden : weights + 2 * hidden]
    tail = bundle_ref[:, weights + 2 * hidden : weights + 2 * hidden + BLK].astype(f32)
    bias = tail[:, 0:1] + tail[:, 1:2] + tail[:, 2:3]
    w_self_all = bundle_ref[:, weights : weights + hidden]
    w_neigh_all = bundle_ref[:, weights + hidden : weights + 2 * hidden]
    contract_rows = (((0,), (0,)), ((), ()))
    width = 8 * BLK
    for start in range(0, slab, width):
        columns = slice(start, start + width)
        preact = (
            lax.dot_general(
                w_self_all, bundle_ref[:, columns], contract_rows, preferred_element_type=f32
            )
            + lax.dot_general(
                w_neigh_all, agg_ref[:, columns], contract_rows, preferred_element_type=f32
            )
            + bias
        )
        s = 1.0 / (1.0 + jnp.exp(-preact))
        silu = preact * s
        out_all[:, columns] = silu.astype(bf16)
        cotangent = bundle_ref[:, slab + start : slab + start + width].astype(f32)
        d_preact = (cotangent * (s + silu * (1.0 - s))).astype(bf16)
        self_ref[:, columns] = jnp.dot(w_self, d_preact, preferred_element_type=f32)
        neigh = jnp.dot(w_neigh, d_preact, preferred_element_type=f32)
        for half in range(width // BLK):
            n = start // BLK + half
            part = neigh[:, half * BLK : (half + 1) * BLK] * inv_ref[n : n + 1]
            scaled[n] = part.astype(bf16)
    out_ref[...] = out_all[pl.ds(first, rows), :]

    zero = jnp.zeros((rows, BLK), bf16)
    contract_columns = (((1,), (1,)), ((), ()))

    def step(k, carry):
        for i in range(chunk):
            t = k * chunk + i
            q = k * (chunk // CAP) + i // CAP
            live = (i % CAP) < counts_ref[0, q]
            chosen = jnp.where(live, scaled[dst_ref[i % CAP, q]], zero)
            start = pl.multiple_of(t * BLK, BLK)
            grads = lax.dot_general(
                chosen, adj_ref[pl.ds(start, BLK), :], contract_columns, preferred_element_type=f32
            )
            grads_ref[t] = grads.astype(bf16)
        return carry

    lax.fori_loop(0, tiles // chunk, step, 0)


def sum_kernel(ids_ref, grads_ref, self_hbm, out_ref, self_ref, sums, sem):
    self_copy = pltpu.make_async_copy(self_hbm, self_ref, sem)
    self_copy.start()
    tiles, rows, _ = grads_ref.shape
    along = ids_ref.shape[0]
    column = tiles // (along * CAP)
    sums[...] = jnp.zeros_like(sums)
    for q in range(tiles // CAP):
        for c in range(CAP):
            block = grads_ref[q * CAP + c].astype(f32)
            sums[c, ids_ref[q // column, c, q % column]] += block
    self_copy.wait()
    for n in range(NB):
        columns = slice(n * BLK, (n + 1) * BLK)
        total = self_ref[:, columns]
        for c in range(CAP):
            total += sums[c, n]
        out_ref[:, columns] = total


def params(limit=VMEM_LIMIT):
    return pltpu.CompilerParams(vmem_limit_bytes=limit)


def shape(dims, dtype):
    return jax.ShapeDtypeStruct(dims, dtype)


def prepare(block_ids, bias, feats, cotangent, w_self, w_neigh, receivers):
    rows, slab = feats.shape
    hidden = w_self.shape[1]
    graph_parts = block_ids.shape[1]
    width = 2 * slab + 2 * hidden + BLK
    return pl.pallas_call(
        prepare_kernel,
        out_shape=(
            shape((rows, slab + CAP * BLK), bf16),
            shape((CAP, BLK), jnp.int32),
            shape((receivers, rows, width), bf16),
        ),
        in_specs=[HBM] * 6,
        out_specs=(VMEM, VMEM, HBM),
        scratch_shapes=[
            pltpu.VMEM((rows, width), bf16),
            pltpu.VMEM((8, BLK), jnp.int32),
            pltpu.VMEM((CAP, graph_parts), jnp.int32),
            pltpu.VMEM((1, rows), f32),
            pltpu.SemaphoreType.DMA((7,)),
            pltpu.SemaphoreType.DMA((receivers,)),
        ],
        compiler_params=params(66_800_000),
        name="prepare",
    )(block_ids, bias, feats, cotangent, w_self, w_neigh)


def select(asked, slabs, along):
    column, rows, _ = slabs.shape
    return pl.pallas_call(
        select_kernel,
        out_shape=shape((along, column * CAP + CAP, rows, BLK), bf16),
        in_specs=[SMEM, VMEM],
        out_specs=VMEM,
        compiler_params=params(),
        name="select_blocks",
    )(asked, slabs)


def aggregate(dst, counts, fetched, adj):
    along, slots, rows, _ = fetched.shape
    tiles = along * (slots - CAP)
    return pl.pallas_call(
        aggregate_kernel,
        out_shape=(shape((rows, NB * BLK), bf16), shape((NB, BLK), f32)),
        in_specs=[HBM, HBM, VMEM, VMEM],
        out_specs=(VMEM, HBM),
        scratch_shapes=[
            pltpu.SMEM(dst.shape, jnp.int32),
            pltpu.SMEM(counts.shape, jnp.int32),
            pltpu.VMEM((NB, BLK), f32),
            pltpu.VMEM((NB + 1, rows + 8, BLK), f32),
            pltpu.SemaphoreType.DMA((3,)),
        ],
        compiler_params=params(),
        name="aggregate",
    )(dst, counts, fetched, adj)


def update(dst, counts, inverse, agg, bundle, adj, rows):
    hidden, slab = agg.shape
    tiles = adj.shape[0] // BLK
    return pl.pallas_call(
        update_kernel,
        out_shape=(
            shape((rows, slab), bf16),
            shape((rows, slab), f32),
            shape((tiles, rows, BLK), bf16),
        ),
        in_specs=[HBM] * 3 + [VMEM, HBM, VMEM],
        out_specs=(VMEM,) * 3,
        scratch_shapes=[
            pltpu.SMEM(dst.shape, jnp.int32),
            pltpu.SMEM(counts.shape, jnp.int32),
            pltpu.VMEM((NB, BLK), f32),
            pltpu.VMEM(bundle.shape, bf16),
            pltpu.VMEM((hidden, slab), bf16),
            pltpu.VMEM((NB, rows, BLK), bf16),
            pltpu.SemaphoreType.DMA((4,)),
        ],
        compiler_params=params(),
        name="update",
    )(dst, counts, inverse, agg, bundle, adj)


def sum_returned(ids, returned, self_grad):
    return pl.pallas_call(
        sum_kernel,
        out_shape=shape(self_grad.shape, f32),
        in_specs=[SMEM, VMEM, HBM],
        out_specs=VMEM,
        scratch_shapes=[
            pltpu.VMEM(self_grad.shape, f32),
            pltpu.VMEM((CAP, NB, returned.shape[1], BLK), f32),
            pltpu.SemaphoreType.DMA,
        ],
        compiler_params=params(),
        name="sum_returned",
    )(ids, returned, self_grad)


def per_device(feats, w_self, w_neigh, bias, cotangent, block_ids, req_counts, tile_dst, adjacency):
    along, column = lax.axis_size("x"), lax.axis_size("z")
    graph_parts = along * column
    hidden = w_self.shape[1]
    rows, slab = feats.shape
    tiles = graph_parts * CAP
    per_row = column * CAP
    adj = adjacency.reshape(tiles * BLK, BLK)
    dst = tile_dst[0].T
    receivers = lax.axis_size("feat")

    packed, ask, bundle = prepare(
        block_ids[0].T, bias.reshape(1, rows), feats, cotangent, w_self, w_neigh, receivers
    )
    bundle = lax.all_to_all(bundle, "feat", 0, 0).reshape(hidden, -1)
    asked = lax.all_gather(ask, "x", axis=0)
    slabs = lax.all_gather(packed, "z", axis=0)
    picked = select(asked, slabs, along)
    picked, bundle = lax.optimization_barrier((picked, bundle))
    fetched = lax.all_to_all(picked, "x", 0, 0)
    agg, inverse = aggregate(dst, req_counts, fetched, adj)
    agg_all = lax.all_gather(agg, "feat", axis=0, tiled=True)
    output, self_grad, grads = update(
        dst, req_counts, inverse, agg_all, bundle, adj, rows
    )
    returned = lax.all_to_all(
        grads.reshape(graph_parts, CAP, rows, BLK), ("x", "z"), 0, 0
    ).reshape(tiles, rows, BLK)
    me = lax.axis_index("x") * column + lax.axis_index("z")
    ids = lax.dynamic_slice(fetched, (0, per_row, 0, me), (along, CAP, rows, 1))
    ids = ids.reshape(along, CAP, rows).astype(jnp.int32)
    feat_grad = sum_returned(ids, returned, self_grad)
    return (output, feat_grad)


def solution(mesh):
    graph, feat = mesh.devices.shape
    along = 4 if graph % 12 == 0 else 2
    mesh = Mesh(mesh.devices.reshape(along, graph // along, feat), ("x", "z", "feat"))
    graph = ("x", "z")
    in_specs = (
        P("feat", graph),
        P("feat", None),
        P("feat", None),
        P("feat"),
        P("feat", graph),
        P(graph, None, None),
        P(graph, None),
        P(graph, None, None),
        P(graph, None, None, None, None),
    )
    out_specs = (P("feat", graph), P("feat", graph))
    return jax.shard_map(
        per_device, mesh=mesh, in_specs=in_specs, out_specs=out_specs, check_vma=False
    )
```

```python
import jax
import jax.numpy as jnp
from jax import lax
from jax.experimental import pallas as pl
from jax.experimental.pallas import tpu as pltpu
from jax.sharding import Mesh, PartitionSpec as P

BLK = 128
NB = 8
CAP = 2
VMEM_LIMIT = 24 * 1024 * 1024

SMEM = pl.BlockSpec(memory_space=pltpu.SMEM)
VMEM = pl.BlockSpec(memory_space=pltpu.VMEM)
HBM = pl.BlockSpec(memory_space=pltpu.HBM)

f32 = jnp.float32
bf16 = jnp.bfloat16


def chunk_of(tiles):
    return 48 if tiles % 48 == 0 else (24 if tiles % 24 == 0 else tiles)


def prepare_kernel(
    ids_hbm,
    bias_hbm,
    feats_hbm,
    cot_hbm,
    w_self_hbm,
    w_neigh_hbm,
    slabs_hbm,
    ask_ref,
    bundle_ref,
    slab_ref,
    ids_ref,
    bias_ref,
    sems,
    out_sems,
):
    rows, slab = feats_hbm.shape
    parts = ids_hbm.shape[1]
    hidden = w_self_hbm.shape[1]
    ends = (slab, slab + hidden, slab + 2 * hidden, slab + 2 * hidden + BLK)
    copies = [
        pltpu.make_async_copy(source, target, sems.at[i])
        for i, (source, target) in enumerate(
            (
                (ids_hbm, ids_ref),
                (feats_hbm, slab_ref.at[:, pl.ds(0, slab)]),
                (bias_hbm, bias_ref),
                (feats_hbm, bundle_ref.at[:, pl.ds(0, slab)]),
                (w_self_hbm, bundle_ref.at[:, pl.ds(ends[0], hidden)]),
                (w_neigh_hbm, bundle_ref.at[:, pl.ds(ends[1], hidden)]),
                (cot_hbm.at[:, pl.ds(0, BLK)], bundle_ref.at[:, pl.ds(ends[3], BLK)]),
            )
        )
    ]
    for copy in copies:
        copy.start()
    ask_ref[...] = jnp.zeros_like(ask_ref)
    copies[0].wait()
    ask_ref[:, 0:parts] = ids_ref[...]
    mine = lax.broadcasted_iota(jnp.int32, (rows, BLK), 0) == lax.axis_index("z")
    for c in range(CAP):
        ids = jnp.broadcast_to(ask_ref[c : c + 1, :], (rows, BLK))
        plane = jnp.where(mine, ids, 0).astype(f32).astype(bf16)
        slab_ref[:, slab + c * BLK : slab + (c + 1) * BLK] = plane
    copies[1].wait()
    out_copies = [
        pltpu.make_async_copy(slab_ref, slabs_hbm.at[i], out_sems.at[i])
        for i in range(slabs_hbm.shape[0])
    ]
    for copy in out_copies:
        copy.start()
    copies[2].wait()
    wide = jnp.broadcast_to(bias_ref[...], (rows, rows))
    place = lax.broadcasted_iota(jnp.int32, (rows, rows), 0)
    place = place == lax.broadcasted_iota(jnp.int32, (rows, rows), 1)
    bias = jnp.sum(jnp.where(place, wide, 0.0), axis=1, keepdims=True)
    high = bias.astype(bf16).astype(f32)
    middle = (bias - high).astype(bf16).astype(f32)
    low = bias - high - middle
    lane = lax.broadcasted_iota(jnp.int32, (rows, BLK), 1)
    terms = jnp.where(lane == 0, high, jnp.where(lane == 1, middle, jnp.where(lane == 2, low, 0.0)))
    bundle_ref[:, ends[2] : ends[3]] = terms.astype(bf16)
    for copy in copies[3:] + out_copies:
        copy.wait()


def select_kernel(ask_ref, slabs_ref, out_ref):
    along, _, rows, _ = out_ref.shape
    column = slabs_ref.shape[0]
    slab = NB * BLK
    first = lax.axis_index("x") * column
    for i in range(along):
        for k in range(column):
            for c in range(CAP):
                start = pl.multiple_of(ask_ref[i, c, first + k] * BLK, BLK)
                out_ref[i, k * CAP + c] = slabs_ref[k, :, pl.ds(start, BLK)]
    for c in range(CAP):
        plane = jnp.zeros((rows, BLK), f32)
        for k in range(column):
            plane += slabs_ref[k, :, slab + c * BLK : slab + (c + 1) * BLK].astype(f32)
        for i in range(along):
            out_ref[i, column * CAP + c] = plane.astype(bf16)


def aggregate_kernel(
    dst_hbm,
    counts_hbm,
    cot_hbm,
    fetched_ref,
    adj_ref,
    agg_ref,
    inv_hbm,
    dst_ref,
    counts_ref,
    inv,
    acc_ref,
    small,
):
    along, slots, rows, _ = fetched_ref.shape
    per_row = slots - CAP
    chunk = chunk_of(per_row)
    dst_copy = pltpu.make_async_copy(dst_hbm, dst_ref, small.at[0])
    counts_copy = pltpu.make_async_copy(counts_hbm, counts_ref, small.at[1])
    dst_copy.start()
    counts_copy.start()
    slab = NB * BLK
    cot_copy = pltpu.make_async_copy(
        cot_hbm.at[:, pl.ds(BLK, slab - BLK)], agg_ref.at[:, pl.ds(slab, slab - BLK)], small.at[3]
    )
    cot_copy.start()
    row_ids = lax.broadcasted_iota(jnp.int32, (16, BLK), 0)
    zero = jnp.zeros((rows, BLK), bf16)
    chunks = per_row // chunk
    dst_copy.wait()
    counts_copy.wait()

    acc_ref[...] = jnp.zeros_like(acc_ref)
    ones = jnp.ones((rows, BLK), bf16)

    def step(k, carry):
        products = []
        for i in range(chunk):
            block = fetched_ref[k // chunks, (k % chunks) * chunk + i]
            start = pl.multiple_of((k * chunk + i) * BLK, BLK)
            products.append(jnp.dot(jnp.concatenate([block, ones], axis=0), adj_ref[pl.ds(start, BLK), :], preferred_element_type=f32))
        for i in range(chunk):
            q = k * (chunk // CAP) + i // CAP
            live = (i % CAP) < counts_ref[0, q]
            dst = jnp.where(live, dst_ref[i % CAP, q], NB)
            acc_ref[dst] += products[i][0 : rows + 8]
        return carry

    lax.fori_loop(0, along * chunks, step, 0)
    for n in range(NB):
        inv[n : n + 1] = 1.0 / jnp.maximum(acc_ref[n, rows : rows + 1], 1.0)
    inv_copy = pltpu.make_async_copy(inv, inv_hbm, small.at[2])
    inv_copy.start()
    for n in range(NB):
        part = acc_ref[n, 0:rows] * inv[n : n + 1]
        agg_ref[:, n * BLK : (n + 1) * BLK] = part.astype(bf16)
    inv_copy.wait()
    cot_copy.wait()


def update_kernel(
    dst_hbm,
    counts_hbm,
    inv_hbm,
    agg_ref,
    bundle_hbm,
    adj_ref,
    out_ref,
    self_ref,
    grads_ref,
    dst_ref,
    counts_ref,
    inv_ref,
    bundle_ref,
    out_all,
    scaled,
    small,
):
    hidden = agg_ref.shape[0]
    slab = NB * BLK
    tiles, rows, _ = grads_ref.shape
    chunk = chunk_of(tiles)
    copies = [
        pltpu.make_async_copy(source, target, small.at[i])
        for i, (source, target) in enumerate(
            (
                (bundle_hbm, bundle_ref),
                (inv_hbm, inv_ref),
                (dst_hbm, dst_ref),
                (counts_hbm, counts_ref),
            )
        )
    ]
    for copy in copies:
        copy.start()
    for copy in copies:
        copy.wait()
    weights = slab
    first = pl.multiple_of(lax.axis_index("feat") * rows, rows)
    w_self = bundle_ref[pl.ds(first, rows), weights : weights + hidden]
    w_neigh = bundle_ref[pl.ds(first, rows), weights + hidden : weights + 2 * hidden]
    tail = bundle_ref[:, weights + 2 * hidden : weights + 2 * hidden + BLK].astype(f32)
    bias = tail[:, 0:1] + tail[:, 1:2] + tail[:, 2:3]
    w_self_all = bundle_ref[:, weights : weights + hidden]
    w_neigh_all = bundle_ref[:, weights + hidden : weights + 2 * hidden]
    contract_rows = (((0,), (0,)), ((), ()))
    width = slab
    for start in range(0, slab, width):
        columns = slice(start, start + width)
        preact = (
            lax.dot_general(
                w_self_all, bundle_ref[:, columns], contract_rows, preferred_element_type=f32
            )
            + lax.dot_general(
                w_neigh_all, agg_ref[:, columns], contract_rows, preferred_element_type=f32
            )
            + bias
        )
        s = 1.0 / (1.0 + jnp.exp(-preact))
        silu = preact * s
        out_all[:, columns] = silu.astype(bf16)
        cotangent = jnp.concatenate(
            [bundle_ref[:, weights + 2 * hidden + BLK :], agg_ref[:, slab:]], axis=1
        ).astype(f32)
        d_preact = (cotangent * (s + silu * (1.0 - s))).astype(bf16)
        self_ref[:, columns] = jnp.dot(w_self, d_preact, preferred_element_type=f32)
        neigh = jnp.dot(w_neigh, d_preact, preferred_element_type=f32)
        for half in range(width // BLK):
            n = start // BLK + half
            part = neigh[:, half * BLK : (half + 1) * BLK] * inv_ref[n : n + 1]
            scaled[n] = part.astype(bf16)
    out_ref[...] = out_all[pl.ds(first, rows), :]

    zero = jnp.zeros((rows, BLK), bf16)
    contract_columns = (((1,), (1,)), ((), ()))

    def step(k, carry):
        for i in range(chunk):
            t = k * chunk + i
            q = k * (chunk // CAP) + i // CAP
            live = (i % CAP) < counts_ref[0, q]
            chosen = jnp.where(live, scaled[dst_ref[i % CAP, q]], zero)
            start = pl.multiple_of(t * BLK, BLK)
            grads = lax.dot_general(
                chosen, adj_ref[pl.ds(start, BLK), :], contract_columns, preferred_element_type=f32
            )
            grads_ref[t] = grads.astype(bf16)
        return carry

    lax.fori_loop(0, tiles // chunk, step, 0)


def sum_kernel(ids_ref, grads_ref, self_hbm, out_ref, self_ref, sums, sem):
    self_copy = pltpu.make_async_copy(self_hbm, self_ref, sem)
    self_copy.start()
    tiles, rows, _ = grads_ref.shape
    along = ids_ref.shape[0]
    column = tiles // (along * CAP)
    sums[...] = jnp.zeros_like(sums)
    for q in range(tiles // CAP):
        for c in range(CAP):
            block = grads_ref[q * CAP + c].astype(f32)
            sums[c, ids_ref[q // column, c, q % column]] += block
    self_copy.wait()
    for n in range(NB):
        columns = slice(n * BLK, (n + 1) * BLK)
        total = self_ref[:, columns]
        for c in range(CAP):
            total += sums[c, n]
        out_ref[:, columns] = total


def params(limit=VMEM_LIMIT):
    return pltpu.CompilerParams(vmem_limit_bytes=limit)


def shape(dims, dtype):
    return jax.ShapeDtypeStruct(dims, dtype)


def prepare(block_ids, bias, feats, cotangent, w_self, w_neigh, receivers):
    rows, slab = feats.shape
    hidden = w_self.shape[1]
    return pl.pallas_call(
        prepare_kernel,
        out_shape=(
            shape((receivers, rows, slab + CAP * BLK), bf16),
            shape((CAP, BLK), jnp.int32),
            shape((rows, slab + 2 * hidden + 2 * BLK), bf16),
        ),
        in_specs=[HBM] * 6,
        out_specs=(HBM, VMEM, VMEM),
        scratch_shapes=[
            pltpu.VMEM((rows, slab + CAP * BLK), bf16),
            pltpu.VMEM(block_ids.shape, jnp.int32),
            pltpu.VMEM((1, rows), f32),
            pltpu.SemaphoreType.DMA((7,)),
            pltpu.SemaphoreType.DMA((receivers,)),
        ],
        compiler_params=params(66_800_000),
        name="prepare",
    )(block_ids, bias, feats, cotangent, w_self, w_neigh)


def select(asked, slabs, along):
    column, rows, _ = slabs.shape
    return pl.pallas_call(
        select_kernel,
        out_shape=shape((along, column * CAP + CAP, rows, BLK), bf16),
        in_specs=[SMEM, VMEM],
        out_specs=VMEM,
        compiler_params=params(),
        name="select_blocks",
    )(asked, slabs)


def aggregate(dst, counts, cotangent, fetched, adj):
    along, slots, rows, _ = fetched.shape
    tiles = along * (slots - CAP)
    return pl.pallas_call(
        aggregate_kernel,
        out_shape=(shape((rows, (2 * NB - 1) * BLK), bf16), shape((NB, BLK), f32)),
        in_specs=[HBM, HBM, HBM, VMEM, VMEM],
        out_specs=(VMEM, HBM),
        scratch_shapes=[
            pltpu.SMEM(dst.shape, jnp.int32),
            pltpu.SMEM(counts.shape, jnp.int32),
            pltpu.VMEM((NB, BLK), f32),
            pltpu.VMEM((NB + 1, rows + 8, BLK), f32),
            pltpu.SemaphoreType.DMA((4,)),
        ],
        compiler_params=params(),
        name="aggregate",
    )(dst, counts, cotangent, fetched, adj)


def update(dst, counts, inverse, agg, bundle, adj, rows):
    hidden, slab = agg.shape[0], NB * BLK
    tiles = adj.shape[0] // BLK
    return pl.pallas_call(
        update_kernel,
        out_shape=(
            shape((rows, slab), bf16),
            shape((rows, slab), f32),
            shape((tiles, rows, BLK), bf16),
        ),
        in_specs=[HBM] * 3 + [VMEM, HBM, VMEM],
        out_specs=(VMEM,) * 3,
        scratch_shapes=[
            pltpu.SMEM(dst.shape, jnp.int32),
            pltpu.SMEM(counts.shape, jnp.int32),
            pltpu.VMEM((NB, BLK), f32),
            pltpu.VMEM(bundle.shape, bf16),
            pltpu.VMEM((hidden, slab), bf16),
            pltpu.VMEM((NB, rows, BLK), bf16),
            pltpu.SemaphoreType.DMA((4,)),
        ],
        compiler_params=params(),
        name="update",
    )(dst, counts, inverse, agg, bundle, adj)


def sum_returned(ids, returned, self_grad):
    return pl.pallas_call(
        sum_kernel,
        out_shape=shape(self_grad.shape, f32),
        in_specs=[SMEM, VMEM, HBM],
        out_specs=VMEM,
        scratch_shapes=[
            pltpu.VMEM(self_grad.shape, f32),
            pltpu.VMEM((CAP, NB, returned.shape[1], BLK), f32),
            pltpu.SemaphoreType.DMA,
        ],
        compiler_params=params(),
        name="sum_returned",
    )(ids, returned, self_grad)


def per_device(feats, w_self, w_neigh, bias, cotangent, block_ids, req_counts, tile_dst, adjacency):
    along, column = lax.axis_size("x"), lax.axis_size("z")
    graph_parts = along * column
    rows, slab = feats.shape
    tiles = graph_parts * CAP
    per_row = column * CAP
    adj = adjacency.reshape(tiles * BLK, BLK)
    dst = tile_dst[0].T

    slabs, ask, bundle = prepare(
        block_ids[0].T, bias.reshape(1, rows), feats, cotangent, w_self, w_neigh, column
    )
    slabs = lax.all_to_all(slabs, "z", 0, 0)
    asked = lax.all_gather(ask, "x", axis=0)
    bundle = lax.all_gather(bundle, "feat", axis=0, tiled=True)
    slabs, asked, bundle = lax.optimization_barrier((slabs, asked, bundle))
    picked = select(asked, slabs, along)
    fetched = lax.all_to_all(picked, "x", 0, 0)
    agg, inverse = aggregate(dst, req_counts, cotangent, fetched, adj)
    agg_all = lax.all_gather(agg, "feat", axis=0, tiled=True)
    output, self_grad, grads = update(
        dst, req_counts, inverse, agg_all, bundle, adj, rows
    )
    returned = lax.all_to_all(
        grads.reshape(graph_parts, CAP, rows, BLK), ("x", "z"), 0, 0
    ).reshape(tiles, rows, BLK)
    me = lax.axis_index("x") * column + lax.axis_index("z")
    ids = lax.dynamic_slice(fetched, (0, per_row, 0, me), (along, CAP, rows, 1))
    ids = ids.reshape(along, CAP, rows).astype(jnp.int32)
    feat_grad = sum_returned(ids, returned, self_grad)
    return (output, feat_grad)


def solution(mesh):
    graph, feat = mesh.devices.shape
    along = 4 if graph % 12 == 0 else 2
    mesh = Mesh(mesh.devices.reshape(along, graph // along, feat), ("x", "z", "feat"))
    graph = ("x", "z")
    in_specs = (
        P("feat", graph),
        P("feat", None),
        P("feat", None),
        P("feat"),
        P("feat", graph),
        P(graph, None, None),
        P(graph, None),
        P(graph, None, None),
        P(graph, None, None, None, None),
    )
    out_specs = (P("feat", graph), P("feat", graph))
    return jax.shard_map(
        per_device, mesh=mesh, in_specs=in_specs, out_specs=out_specs, check_vma=False
    )
```

```python
import jax
import jax.numpy as jnp
from jax import lax
from jax.experimental import pallas as pl
from jax.experimental.pallas import tpu as pltpu
from jax.sharding import Mesh, PartitionSpec as P

BLK = 128
NB = 8
CAP = 2
VMEM_LIMIT = 24 * 1024 * 1024

SMEM = pl.BlockSpec(memory_space=pltpu.SMEM)
VMEM = pl.BlockSpec(memory_space=pltpu.VMEM)
HBM = pl.BlockSpec(memory_space=pltpu.HBM)

f32 = jnp.float32
bf16 = jnp.bfloat16


def chunk_of(tiles):
    return 48 if tiles % 48 == 0 else (24 if tiles % 24 == 0 else tiles)


def prepare_kernel(
    ids_hbm,
    bias_hbm,
    feats_hbm,
    cot_hbm,
    w_self_hbm,
    w_neigh_hbm,
    slabs_hbm,
    ask_ref,
    bundle_ref,
    slab_ref,
    ids_ref,
    bias_ref,
    sems,
    out_sems,
):
    rows, slab = feats_hbm.shape
    parts = ids_hbm.shape[1]
    hidden = w_self_hbm.shape[1]
    ends = (slab, slab + hidden, slab + 2 * hidden, slab + 2 * hidden + BLK)
    copies = [
        pltpu.make_async_copy(source, target, sems.at[i])
        for i, (source, target) in enumerate(
            (
                (ids_hbm, ids_ref),
                (feats_hbm, slab_ref.at[:, pl.ds(0, slab)]),
                (bias_hbm, bias_ref),
                (feats_hbm, bundle_ref.at[:, pl.ds(0, slab)]),
                (w_self_hbm, bundle_ref.at[:, pl.ds(ends[0], hidden)]),
                (w_neigh_hbm, bundle_ref.at[:, pl.ds(ends[1], hidden)]),
                (cot_hbm.at[:, pl.ds(0, BLK)], bundle_ref.at[:, pl.ds(ends[3], BLK)]),
            )
        )
    ]
    for copy in copies:
        copy.start()
    ask_ref[...] = jnp.zeros_like(ask_ref)
    copies[0].wait()
    ask_ref[:, 0:parts] = ids_ref[...]
    mine = lax.broadcasted_iota(jnp.int32, (rows, BLK), 0) == lax.axis_index("z")
    for c in range(CAP):
        ids = jnp.broadcast_to(ask_ref[c : c + 1, :], (rows, BLK))
        plane = jnp.where(mine, ids, 0).astype(f32).astype(bf16)
        slab_ref[:, slab + c * BLK : slab + (c + 1) * BLK] = plane
    copies[1].wait()
    out_copies = [
        pltpu.make_async_copy(slab_ref, slabs_hbm.at[i], out_sems.at[i])
        for i in range(slabs_hbm.shape[0])
    ]
    for copy in out_copies:
        copy.start()
    copies[2].wait()
    wide = jnp.broadcast_to(bias_ref[...], (rows, rows))
    place = lax.broadcasted_iota(jnp.int32, (rows, rows), 0)
    place = place == lax.broadcasted_iota(jnp.int32, (rows, rows), 1)
    bias = jnp.sum(jnp.where(place, wide, 0.0), axis=1, keepdims=True)
    high = bias.astype(bf16).astype(f32)
    middle = (bias - high).astype(bf16).astype(f32)
    low = bias - high - middle
    lane = lax.broadcasted_iota(jnp.int32, (rows, BLK), 1)
    terms = jnp.where(lane == 0, high, jnp.where(lane == 1, middle, jnp.where(lane == 2, low, 0.0)))
    bundle_ref[:, ends[2] : ends[3]] = terms.astype(bf16)
    for copy in copies[3:] + out_copies:
        copy.wait()


def select_kernel(ask_ref, slabs_ref, out_ref):
    along, _, rows, _ = out_ref.shape
    column = slabs_ref.shape[0]
    slab = NB * BLK
    first = lax.axis_index("x") * column
    for i in range(along):
        for k in range(column):
            for c in range(CAP):
                start = pl.multiple_of(ask_ref[i, c, first + k] * BLK, BLK)
                out_ref[i, k * CAP + c] = slabs_ref[k, :, pl.ds(start, BLK)]
    for c in range(CAP):
        plane = jnp.zeros((rows, BLK), f32)
        for k in range(column):
            plane += slabs_ref[k, :, slab + c * BLK : slab + (c + 1) * BLK].astype(f32)
        for i in range(along):
            out_ref[i, column * CAP + c] = plane.astype(bf16)


def aggregate_kernel(
    dst_hbm,
    counts_hbm,
    cot_hbm,
    fetched_ref,
    adj_ref,
    agg_ref,
    inv_hbm,
    dst_ref,
    counts_ref,
    inv,
    acc_ref,
    small,
):
    along, slots, rows, _ = fetched_ref.shape
    per_row = slots - CAP
    chunk = chunk_of(per_row)
    dst_copy = pltpu.make_async_copy(dst_hbm, dst_ref, small.at[0])
    counts_copy = pltpu.make_async_copy(counts_hbm, counts_ref, small.at[1])
    dst_copy.start()
    counts_copy.start()
    slab = NB * BLK
    cot_copy = pltpu.make_async_copy(
        cot_hbm.at[:, pl.ds(BLK, slab - BLK)], agg_ref.at[:, pl.ds(slab, slab - BLK)], small.at[3]
    )
    cot_copy.start()
    row_ids = lax.broadcasted_iota(jnp.int32, (16, BLK), 0)
    zero = jnp.zeros((rows, BLK), bf16)
    chunks = per_row // chunk
    dst_copy.wait()
    counts_copy.wait()

    acc_ref[...] = jnp.zeros_like(acc_ref)
    ones = jnp.ones((rows, BLK), bf16)

    def step(k, carry):
        products = []
        for i in range(chunk):
            block = fetched_ref[k // chunks, (k % chunks) * chunk + i]
            start = pl.multiple_of((k * chunk + i) * BLK, BLK)
            products.append(jnp.dot(jnp.concatenate([block, ones], axis=0), adj_ref[pl.ds(start, BLK), :], preferred_element_type=f32))
        for i in range(chunk):
            q = k * (chunk // CAP) + i // CAP
            live = (i % CAP) < counts_ref[0, q]
            dst = jnp.where(live, dst_ref[i % CAP, q], NB)
            acc_ref[dst] += products[i][0 : rows + 8]
        return carry

    lax.fori_loop(0, along * chunks, step, 0)
    for n in range(NB):
        inv[n : n + 1] = 1.0 / jnp.maximum(acc_ref[n, rows : rows + 1], 1.0)
    inv_copy = pltpu.make_async_copy(inv, inv_hbm, small.at[2])
    inv_copy.start()
    for n in range(NB):
        part = acc_ref[n, 0:rows] * inv[n : n + 1]
        agg_ref[:, n * BLK : (n + 1) * BLK] = part.astype(bf16)
    inv_copy.wait()
    cot_copy.wait()


def update_kernel(
    dst_hbm,
    counts_hbm,
    inv_hbm,
    agg_ref,
    bundle_hbm,
    adj_ref,
    out_ref,
    self_ref,
    grads_ref,
    dst_ref,
    counts_ref,
    inv_ref,
    bundle_ref,
    out_all,
    scaled,
    small,
):
    hidden = agg_ref.shape[0]
    slab = NB * BLK
    tiles, rows, _ = grads_ref.shape
    chunk = chunk_of(tiles)
    copies = [
        pltpu.make_async_copy(source, target, small.at[i])
        for i, (source, target) in enumerate(
            (
                (bundle_hbm, bundle_ref),
                (inv_hbm, inv_ref),
                (dst_hbm, dst_ref),
                (counts_hbm, counts_ref),
            )
        )
    ]
    for copy in copies:
        copy.start()
    for copy in copies:
        copy.wait()
    weights = slab
    first = pl.multiple_of(lax.axis_index("feat") * rows, rows)
    w_self = bundle_ref[pl.ds(first, rows), weights : weights + hidden]
    w_neigh = bundle_ref[pl.ds(first, rows), weights + hidden : weights + 2 * hidden]
    tail = bundle_ref[:, weights + 2 * hidden : weights + 2 * hidden + BLK].astype(f32)
    bias = tail[:, 0:1] + tail[:, 1:2] + tail[:, 2:3]
    w_self_all = bundle_ref[:, weights : weights + hidden]
    w_neigh_all = bundle_ref[:, weights + hidden : weights + 2 * hidden]
    contract_rows = (((0,), (0,)), ((), ()))
    width = slab
    for start in range(0, slab, width):
        columns = slice(start, start + width)
        preact = (
            lax.dot_general(
                w_self_all, bundle_ref[:, columns], contract_rows, preferred_element_type=f32
            )
            + lax.dot_general(
                w_neigh_all, agg_ref[:, columns], contract_rows, preferred_element_type=f32
            )
            + bias
        )
        s = 1.0 / (1.0 + jnp.exp(-preact))
        silu = preact * s
        out_all[:, columns] = silu.astype(bf16)
        cotangent = jnp.concatenate(
            [bundle_ref[:, weights + 2 * hidden + BLK :], agg_ref[:, slab:]], axis=1
        ).astype(f32)
        d_preact = (cotangent * (s + silu * (1.0 - s))).astype(bf16)
        self_ref[:, columns] = jnp.dot(w_self, d_preact, preferred_element_type=f32)
        neigh = jnp.dot(w_neigh, d_preact, preferred_element_type=f32)
        for half in range(width // BLK):
            n = start // BLK + half
            part = neigh[:, half * BLK : (half + 1) * BLK] * inv_ref[n : n + 1]
            scaled[n] = part.astype(bf16)
    out_ref[...] = out_all[pl.ds(first, rows), :]

    zero = jnp.zeros((rows, BLK), bf16)
    contract_columns = (((1,), (1,)), ((), ()))

    def step(k, carry):
        for i in range(chunk):
            t = k * chunk + i
            q = k * (chunk // CAP) + i // CAP
            live = (i % CAP) < counts_ref[0, q]
            chosen = jnp.where(live, scaled[dst_ref[i % CAP, q]], zero)
            start = pl.multiple_of(t * BLK, BLK)
            grads = lax.dot_general(
                chosen, adj_ref[pl.ds(start, BLK), :], contract_columns, preferred_element_type=f32
            )
            grads_ref[t] = grads.astype(bf16)
        return carry

    lax.fori_loop(0, tiles // chunk, step, 0)


def sum_kernel(ids_ref, grads_ref, self_hbm, out_ref, self_ref, sums, sem):
    self_copy = pltpu.make_async_copy(self_hbm, self_ref, sem)
    self_copy.start()
    tiles, rows, _ = grads_ref.shape
    along = ids_ref.shape[0]
    column = tiles // (along * CAP)
    sums[...] = jnp.zeros_like(sums)
    for q in range(tiles // CAP):
        for c in range(CAP):
            block = grads_ref[q * CAP + c].astype(f32)
            sums[c, ids_ref[q // column, c, q % column]] += block
    self_copy.wait()
    for n in range(NB):
        columns = slice(n * BLK, (n + 1) * BLK)
        total = self_ref[:, columns]
        for c in range(CAP):
            total += sums[c, n]
        out_ref[:, columns] = total


def params(limit=VMEM_LIMIT):
    return pltpu.CompilerParams(vmem_limit_bytes=limit)


def shape(dims, dtype):
    return jax.ShapeDtypeStruct(dims, dtype)


def prepare(block_ids, bias, feats, cotangent, w_self, w_neigh, receivers):
    rows, slab = feats.shape
    hidden = w_self.shape[1]
    return pl.pallas_call(
        prepare_kernel,
        out_shape=(
            shape((receivers, rows, slab + CAP * BLK), bf16),
            shape((CAP, BLK), jnp.int32),
            shape((rows, slab + 2 * hidden + 2 * BLK), bf16),
        ),
        in_specs=[HBM] * 6,
        out_specs=(HBM, VMEM, VMEM),
        scratch_shapes=[
            pltpu.VMEM((rows, slab + CAP * BLK), bf16),
            pltpu.VMEM(block_ids.shape, jnp.int32),
            pltpu.VMEM((1, rows), f32),
            pltpu.SemaphoreType.DMA((7,)),
            pltpu.SemaphoreType.DMA((receivers,)),
        ],
        compiler_params=params(66_800_000),
        name="prepare",
    )(block_ids, bias, feats, cotangent, w_self, w_neigh)


def select(asked, slabs, along):
    column, rows, _ = slabs.shape
    return pl.pallas_call(
        select_kernel,
        out_shape=shape((along, column * CAP + CAP, rows, BLK), bf16),
        in_specs=[SMEM, VMEM],
        out_specs=VMEM,
        compiler_params=params(),
        name="select_blocks",
    )(asked, slabs)


def aggregate(dst, counts, cotangent, fetched, adj):
    along, slots, rows, _ = fetched.shape
    tiles = along * (slots - CAP)
    return pl.pallas_call(
        aggregate_kernel,
        out_shape=(shape((rows, (2 * NB - 1) * BLK), bf16), shape((NB, BLK), f32)),
        in_specs=[HBM, HBM, HBM, VMEM, VMEM],
        out_specs=(VMEM, HBM),
        scratch_shapes=[
            pltpu.SMEM(dst.shape, jnp.int32),
            pltpu.SMEM(counts.shape, jnp.int32),
            pltpu.VMEM((NB, BLK), f32),
            pltpu.VMEM((NB + 1, rows + 8, BLK), f32),
            pltpu.SemaphoreType.DMA((4,)),
        ],
        compiler_params=params(),
        name="aggregate",
    )(dst, counts, cotangent, fetched, adj)


def update(dst, counts, inverse, agg, bundle, adj, rows):
    hidden, slab = agg.shape[0], NB * BLK
    tiles = adj.shape[0] // BLK
    return pl.pallas_call(
        update_kernel,
        out_shape=(
            shape((rows, slab), bf16),
            shape((rows, slab), f32),
            shape((tiles, rows, BLK), bf16),
        ),
        in_specs=[HBM] * 3 + [VMEM, HBM, VMEM],
        out_specs=(VMEM,) * 3,
        scratch_shapes=[
            pltpu.SMEM(dst.shape, jnp.int32),
            pltpu.SMEM(counts.shape, jnp.int32),
            pltpu.VMEM((NB, BLK), f32),
            pltpu.VMEM(bundle.shape, bf16),
            pltpu.VMEM((hidden, slab), bf16),
            pltpu.VMEM((NB, rows, BLK), bf16),
            pltpu.SemaphoreType.DMA((4,)),
        ],
        compiler_params=params(),
        name="update",
    )(dst, counts, inverse, agg, bundle, adj)


def sum_returned(ids, returned, self_grad):
    return pl.pallas_call(
        sum_kernel,
        out_shape=shape(self_grad.shape, f32),
        in_specs=[SMEM, VMEM, HBM],
        out_specs=VMEM,
        scratch_shapes=[
            pltpu.VMEM(self_grad.shape, f32),
            pltpu.VMEM((CAP, NB, returned.shape[1], BLK), f32),
            pltpu.SemaphoreType.DMA,
        ],
        compiler_params=params(),
        name="sum_returned",
    )(ids, returned, self_grad)


def per_device(feats, w_self, w_neigh, bias, cotangent, block_ids, req_counts, tile_dst, adjacency):
    along, column = lax.axis_size("x"), lax.axis_size("z")
    graph_parts = along * column
    rows, slab = feats.shape
    tiles = graph_parts * CAP
    per_row = column * CAP
    adj = adjacency.reshape(tiles * BLK, BLK)
    dst = tile_dst[0].T

    slabs, ask, bundle = prepare(
        block_ids[0].T, bias.reshape(1, rows), feats, cotangent, w_self, w_neigh, column
    )
    slabs = lax.all_to_all(slabs, "z", 0, 0)
    asked = lax.all_gather(ask, "x", axis=0)
    slabs, asked = lax.optimization_barrier((slabs, asked))
    picked = select(asked, slabs, along)
    picked, bundle = lax.optimization_barrier((picked, bundle))
    fetched = lax.all_to_all(picked, "x", 0, 0)
    bundle = lax.all_gather(bundle, "feat", axis=0, tiled=True)
    fetched, bundle = lax.optimization_barrier((fetched, bundle))
    agg, inverse = aggregate(dst, req_counts, cotangent, fetched, adj)
    agg_all = lax.all_gather(agg, "feat", axis=0, tiled=True)
    output, self_grad, grads = update(
        dst, req_counts, inverse, agg_all, bundle, adj, rows
    )
    returned = lax.all_to_all(
        grads.reshape(graph_parts, CAP, rows, BLK), ("x", "z"), 0, 0
    ).reshape(tiles, rows, BLK)
    me = lax.axis_index("x") * column + lax.axis_index("z")
    ids = lax.dynamic_slice(fetched, (0, per_row, 0, me), (along, CAP, rows, 1))
    ids = ids.reshape(along, CAP, rows).astype(jnp.int32)
    feat_grad = sum_returned(ids, returned, self_grad)
    return (output, feat_grad)


def solution(mesh):
    graph, feat = mesh.devices.shape
    along = 4 if graph % 12 == 0 else 2
    mesh = Mesh(mesh.devices.reshape(along, graph // along, feat), ("x", "z", "feat"))
    graph = ("x", "z")
    in_specs = (
        P("feat", graph),
        P("feat", None),
        P("feat", None),
        P("feat"),
        P("feat", graph),
        P(graph, None, None),
        P(graph, None),
        P(graph, None, None),
        P(graph, None, None, None, None),
    )
    out_specs = (P("feat", graph), P("feat", graph))
    return jax.shard_map(
        per_device, mesh=mesh, in_specs=in_specs, out_specs=out_specs, check_vma=False
    )
```

```python
import jax
import jax.numpy as jnp
from jax import lax
from jax.experimental import pallas as pl
from jax.experimental.pallas import tpu as pltpu
from jax.sharding import Mesh, PartitionSpec as P

BLK = 128
NB = 8
CAP = 2
VMEM_LIMIT = 24 * 1024 * 1024

SMEM = pl.BlockSpec(memory_space=pltpu.SMEM)
VMEM = pl.BlockSpec(memory_space=pltpu.VMEM)
HBM = pl.BlockSpec(memory_space=pltpu.HBM)

f32 = jnp.float32
bf16 = jnp.bfloat16


def chunk_of(tiles):
    return 48 if tiles % 48 == 0 else (24 if tiles % 24 == 0 else tiles)


def prepare_kernel(
    ids_hbm,
    bias_hbm,
    feats_hbm,
    cot_hbm,
    w_self_hbm,
    w_neigh_hbm,
    slabs_hbm,
    ask_ref,
    bundle_ref,
    slab_ref,
    ids_ref,
    bias_ref,
    sems,
    out_sems,
):
    rows, slab = feats_hbm.shape
    parts = ids_hbm.shape[1]
    hidden = w_self_hbm.shape[1]
    ends = (slab, slab + hidden, slab + 2 * hidden, slab + 2 * hidden + BLK)
    copies = [
        pltpu.make_async_copy(source, target, sems.at[i])
        for i, (source, target) in enumerate(
            (
                (ids_hbm, ids_ref),
                (feats_hbm, slab_ref.at[:, pl.ds(0, slab)]),
                (bias_hbm, bias_ref),
                (feats_hbm, bundle_ref.at[:, pl.ds(0, slab)]),
                (w_self_hbm, bundle_ref.at[:, pl.ds(ends[0], hidden)]),
                (w_neigh_hbm, bundle_ref.at[:, pl.ds(ends[1], hidden)]),
                (cot_hbm.at[:, pl.ds(0, BLK)], bundle_ref.at[:, pl.ds(ends[3], BLK)]),
            )
        )
    ]
    for copy in copies:
        copy.start()
    ask_ref[...] = jnp.zeros_like(ask_ref)
    copies[0].wait()
    ask_ref[:, 0:parts] = ids_ref[...]
    mine = lax.broadcasted_iota(jnp.int32, (rows, BLK), 0) == lax.axis_index("z")
    for c in range(CAP):
        ids = jnp.broadcast_to(ask_ref[c : c + 1, :], (rows, BLK))
        plane = jnp.where(mine, ids, 0).astype(f32).astype(bf16)
        slab_ref[:, slab + c * BLK : slab + (c + 1) * BLK] = plane
    copies[1].wait()
    out_copies = [
        pltpu.make_async_copy(slab_ref, slabs_hbm.at[i], out_sems.at[i])
        for i in range(slabs_hbm.shape[0])
    ]
    for copy in out_copies:
        copy.start()
    copies[2].wait()
    wide = jnp.broadcast_to(bias_ref[...], (rows, rows))
    place = lax.broadcasted_iota(jnp.int32, (rows, rows), 0)
    place = place == lax.broadcasted_iota(jnp.int32, (rows, rows), 1)
    bias = jnp.sum(jnp.where(place, wide, 0.0), axis=1, keepdims=True)
    high = bias.astype(bf16).astype(f32)
    middle = (bias - high).astype(bf16).astype(f32)
    low = bias - high - middle
    lane = lax.broadcasted_iota(jnp.int32, (rows, BLK), 1)
    terms = jnp.where(lane == 0, high, jnp.where(lane == 1, middle, jnp.where(lane == 2, low, 0.0)))
    bundle_ref[:, ends[2] : ends[3]] = terms.astype(bf16)
    for copy in copies[3:] + out_copies:
        copy.wait()


def select_kernel(ask_ref, slabs_ref, out_ref):
    along, _, rows, _ = out_ref.shape
    column = slabs_ref.shape[0]
    slab = NB * BLK
    first = lax.axis_index("x") * column
    for i in range(along):
        for k in range(column):
            for c in range(CAP):
                start = pl.multiple_of(ask_ref[i, c, first + k] * BLK, BLK)
                out_ref[i, k * CAP + c] = slabs_ref[k, :, pl.ds(start, BLK)]
    for c in range(CAP):
        plane = jnp.zeros((rows, BLK), f32)
        for k in range(column):
            plane += slabs_ref[k, :, slab + c * BLK : slab + (c + 1) * BLK].astype(f32)
        for i in range(along):
            out_ref[i, column * CAP + c] = plane.astype(bf16)


def aggregate_kernel(
    dst_hbm,
    counts_hbm,
    cot_hbm,
    fetched_ref,
    adj_ref,
    agg_ref,
    inv_hbm,
    dst_ref,
    counts_ref,
    inv,
    acc_ref,
    small,
):
    along, slots, rows, _ = fetched_ref.shape
    per_row = slots - CAP
    chunk = chunk_of(per_row)
    dst_copy = pltpu.make_async_copy(dst_hbm, dst_ref, small.at[0])
    counts_copy = pltpu.make_async_copy(counts_hbm, counts_ref, small.at[1])
    dst_copy.start()
    counts_copy.start()
    slab = NB * BLK
    cot_copy = pltpu.make_async_copy(
        cot_hbm.at[:, pl.ds(BLK, slab - BLK)], agg_ref.at[:, pl.ds(slab, slab - BLK)], small.at[3]
    )
    cot_copy.start()
    row_ids = lax.broadcasted_iota(jnp.int32, (16, BLK), 0)
    zero = jnp.zeros((rows, BLK), bf16)
    chunks = per_row // chunk
    dst_copy.wait()
    counts_copy.wait()

    acc_ref[...] = jnp.zeros_like(acc_ref)
    ones = jnp.ones((rows, BLK), bf16)

    def step(k, carry):
        products = []
        for i in range(chunk):
            block = fetched_ref[k // chunks, (k % chunks) * chunk + i]
            start = pl.multiple_of((k * chunk + i) * BLK, BLK)
            products.append(jnp.dot(jnp.concatenate([block, ones], axis=0), adj_ref[pl.ds(start, BLK), :], preferred_element_type=f32))
        for i in range(chunk):
            q = k * (chunk // CAP) + i // CAP
            live = (i % CAP) < counts_ref[0, q]
            dst = jnp.where(live, dst_ref[i % CAP, q], NB)
            acc_ref[dst] += products[i][0 : rows + 8]
        return carry

    lax.fori_loop(0, along * chunks, step, 0)
    for n in range(NB):
        inv[n : n + 1] = 1.0 / jnp.maximum(acc_ref[n, rows : rows + 1], 1.0)
    inv_copy = pltpu.make_async_copy(inv, inv_hbm, small.at[2])
    inv_copy.start()
    for n in range(NB):
        part = acc_ref[n, 0:rows] * inv[n : n + 1]
        agg_ref[:, n * BLK : (n + 1) * BLK] = part.astype(bf16)
    inv_copy.wait()
    cot_copy.wait()


def update_kernel(
    dst_hbm,
    counts_hbm,
    inv_hbm,
    agg_ref,
    bundle_hbm,
    adj_ref,
    out_ref,
    self_ref,
    grads_ref,
    dst_ref,
    counts_ref,
    inv_ref,
    bundle_ref,
    out_all,
    scaled,
    small,
):
    hidden = agg_ref.shape[0]
    slab = NB * BLK
    tiles, rows, _ = grads_ref.shape
    chunk = chunk_of(tiles)
    copies = [
        pltpu.make_async_copy(source, target, small.at[i])
        for i, (source, target) in enumerate(
            (
                (bundle_hbm, bundle_ref),
                (inv_hbm, inv_ref),
                (dst_hbm, dst_ref),
                (counts_hbm, counts_ref),
            )
        )
    ]
    for copy in copies:
        copy.start()
    for copy in copies:
        copy.wait()
    weights = slab
    first = pl.multiple_of(lax.axis_index("feat") * rows, rows)
    w_self = bundle_ref[pl.ds(first, rows), weights : weights + hidden]
    w_neigh = bundle_ref[pl.ds(first, rows), weights + hidden : weights + 2 * hidden]
    tail = bundle_ref[:, weights + 2 * hidden : weights + 2 * hidden + BLK].astype(f32)
    bias = tail[:, 0:1] + tail[:, 1:2] + tail[:, 2:3]
    w_self_all = bundle_ref[:, weights : weights + hidden]
    w_neigh_all = bundle_ref[:, weights + hidden : weights + 2 * hidden]
    contract_rows = (((0,), (0,)), ((), ()))
    width = slab
    for start in range(0, slab, width):
        columns = slice(start, start + width)
        preact = (
            lax.dot_general(
                w_self_all, bundle_ref[:, columns], contract_rows, preferred_element_type=f32
            )
            + lax.dot_general(
                w_neigh_all, agg_ref[:, columns], contract_rows, preferred_element_type=f32
            )
            + bias
        )
        s = 1.0 / (1.0 + jnp.exp(-preact))
        silu = preact * s
        out_all[:, columns] = silu.astype(bf16)
        cotangent = jnp.concatenate(
            [bundle_ref[:, weights + 2 * hidden + BLK :], agg_ref[:, slab:]], axis=1
        ).astype(f32)
        d_preact = (cotangent * (s + silu * (1.0 - s))).astype(bf16)
        self_ref[:, columns] = jnp.dot(w_self, d_preact, preferred_element_type=f32)
        neigh = jnp.dot(w_neigh, d_preact, preferred_element_type=f32)
        for half in range(width // BLK):
            n = start // BLK + half
            part = neigh[:, half * BLK : (half + 1) * BLK] * inv_ref[n : n + 1]
            scaled[n] = part.astype(bf16)
    out_ref[...] = out_all[pl.ds(first, rows), :]

    zero = jnp.zeros((rows, BLK), bf16)
    contract_columns = (((1,), (1,)), ((), ()))

    def step(k, carry):
        for i in range(chunk):
            t = k * chunk + i
            q = k * (chunk // CAP) + i // CAP
            live = (i % CAP) < counts_ref[0, q]
            chosen = jnp.where(live, scaled[dst_ref[i % CAP, q]], zero)
            start = pl.multiple_of(t * BLK, BLK)
            grads = lax.dot_general(
                chosen, adj_ref[pl.ds(start, BLK), :], contract_columns, preferred_element_type=f32
            )
            grads_ref[t] = grads.astype(bf16)
        return carry

    lax.fori_loop(0, tiles // chunk, step, 0)


def sum_kernel(ids_ref, grads_ref, self_hbm, out_ref, self_ref, sums, sem):
    self_copy = pltpu.make_async_copy(self_hbm, self_ref, sem)
    self_copy.start()
    tiles, rows, _ = grads_ref.shape
    along = ids_ref.shape[0]
    column = tiles // (along * CAP)
    sums[...] = jnp.zeros_like(sums)
    for q in range(tiles // CAP):
        for c in range(CAP):
            block = grads_ref[q * CAP + c].astype(f32)
            sums[c, ids_ref[q // column, c, q % column]] += block
    self_copy.wait()
    for n in range(NB):
        columns = slice(n * BLK, (n + 1) * BLK)
        total = self_ref[:, columns]
        for c in range(CAP):
            total += sums[c, n]
        out_ref[:, columns] = total


def params(limit=VMEM_LIMIT):
    return pltpu.CompilerParams(vmem_limit_bytes=limit)


def shape(dims, dtype):
    return jax.ShapeDtypeStruct(dims, dtype)


def prepare(block_ids, bias, feats, cotangent, w_self, w_neigh, receivers):
    rows, slab = feats.shape
    hidden = w_self.shape[1]
    return pl.pallas_call(
        prepare_kernel,
        out_shape=(
            shape((receivers, rows, slab + CAP * BLK), bf16),
            shape((CAP, BLK), jnp.int32),
            shape((rows, slab + 2 * hidden + 2 * BLK), bf16),
        ),
        in_specs=[HBM] * 6,
        out_specs=(HBM, VMEM, VMEM),
        scratch_shapes=[
            pltpu.VMEM((rows, slab + CAP * BLK), bf16),
            pltpu.VMEM(block_ids.shape, jnp.int32),
            pltpu.VMEM((1, rows), f32),
            pltpu.SemaphoreType.DMA((7,)),
            pltpu.SemaphoreType.DMA((receivers,)),
        ],
        compiler_params=params(66_800_000),
        name="prepare",
    )(block_ids, bias, feats, cotangent, w_self, w_neigh)


def select(asked, slabs, along):
    column, rows, _ = slabs.shape
    return pl.pallas_call(
        select_kernel,
        out_shape=shape((along, column * CAP + CAP, rows, BLK), bf16),
        in_specs=[SMEM, VMEM],
        out_specs=VMEM,
        compiler_params=params(),
        name="select_blocks",
    )(asked, slabs)


def aggregate(dst, counts, cotangent, fetched, adj):
    along, slots, rows, _ = fetched.shape
    tiles = along * (slots - CAP)
    return pl.pallas_call(
        aggregate_kernel,
        out_shape=(shape((rows, (2 * NB - 1) * BLK), bf16), shape((NB, BLK), f32)),
        in_specs=[HBM, HBM, HBM, VMEM, VMEM],
        out_specs=(VMEM, HBM),
        scratch_shapes=[
            pltpu.SMEM(dst.shape, jnp.int32),
            pltpu.SMEM(counts.shape, jnp.int32),
            pltpu.VMEM((NB, BLK), f32),
            pltpu.VMEM((NB + 1, rows + 8, BLK), f32),
            pltpu.SemaphoreType.DMA((4,)),
        ],
        compiler_params=params(),
        name="aggregate",
    )(dst, counts, cotangent, fetched, adj)


def update(dst, counts, inverse, agg, bundle, adj, rows):
    hidden, slab = agg.shape[0], NB * BLK
    tiles = adj.shape[0] // BLK
    return pl.pallas_call(
        update_kernel,
        out_shape=(
            shape((rows, slab), bf16),
            shape((rows, slab), f32),
            shape((tiles, rows, BLK), bf16),
        ),
        in_specs=[HBM] * 3 + [VMEM, HBM, VMEM],
        out_specs=(VMEM,) * 3,
        scratch_shapes=[
            pltpu.SMEM(dst.shape, jnp.int32),
            pltpu.SMEM(counts.shape, jnp.int32),
            pltpu.VMEM((NB, BLK), f32),
            pltpu.VMEM(bundle.shape, bf16),
            pltpu.VMEM((hidden, slab), bf16),
            pltpu.VMEM((NB, rows, BLK), bf16),
            pltpu.SemaphoreType.DMA((4,)),
        ],
        compiler_params=params(),
        name="update",
    )(dst, counts, inverse, agg, bundle, adj)


def sum_returned(ids, returned, self_grad):
    return pl.pallas_call(
        sum_kernel,
        out_shape=shape(self_grad.shape, f32),
        in_specs=[SMEM, VMEM, HBM],
        out_specs=VMEM,
        scratch_shapes=[
            pltpu.VMEM(self_grad.shape, f32),
            pltpu.VMEM((CAP, NB, returned.shape[1], BLK), f32),
            pltpu.SemaphoreType.DMA,
        ],
        compiler_params=params(),
        name="sum_returned",
    )(ids, returned, self_grad)


def per_device(feats, w_self, w_neigh, bias, cotangent, block_ids, req_counts, tile_dst, adjacency):
    along, column = lax.axis_size("x"), lax.axis_size("z")
    graph_parts = along * column
    rows, slab = feats.shape
    tiles = graph_parts * CAP
    per_row = column * CAP
    adj = adjacency.reshape(tiles * BLK, BLK)
    dst = tile_dst[0].T

    slabs, ask, bundle = prepare(
        block_ids[0].T, bias.reshape(1, rows), feats, cotangent, w_self, w_neigh, column
    )
    asked = lax.all_gather(ask, "x", axis=0)
    slabs, bundle, asked = lax.optimization_barrier((slabs, bundle, asked))
    slabs = lax.all_to_all(slabs, "z", 0, 0)
    bundle = lax.all_gather(bundle, "feat", axis=0, tiled=True)
    slabs, bundle = lax.optimization_barrier((slabs, bundle))
    picked = select(asked, slabs, along)
    fetched = lax.all_to_all(picked, "x", 0, 0)
    agg, inverse = aggregate(dst, req_counts, cotangent, fetched, adj)
    agg_all = lax.all_gather(agg, "feat", axis=0, tiled=True)
    output, self_grad, grads = update(
        dst, req_counts, inverse, agg_all, bundle, adj, rows
    )
    returned = lax.all_to_all(
        grads.reshape(graph_parts, CAP, rows, BLK), ("x", "z"), 0, 0
    ).reshape(tiles, rows, BLK)
    me = lax.axis_index("x") * column + lax.axis_index("z")
    ids = lax.dynamic_slice(fetched, (0, per_row, 0, me), (along, CAP, rows, 1))
    ids = ids.reshape(along, CAP, rows).astype(jnp.int32)
    feat_grad = sum_returned(ids, returned, self_grad)
    return (output, feat_grad)


def solution(mesh):
    graph, feat = mesh.devices.shape
    along = 4 if graph % 12 == 0 else 2
    mesh = Mesh(mesh.devices.reshape(along, graph // along, feat), ("x", "z", "feat"))
    graph = ("x", "z")
    in_specs = (
        P("feat", graph),
        P("feat", None),
        P("feat", None),
        P("feat"),
        P("feat", graph),
        P(graph, None, None),
        P(graph, None),
        P(graph, None, None),
        P(graph, None, None, None, None),
    )
    out_specs = (P("feat", graph), P("feat", graph))
    return jax.shard_map(
        per_device, mesh=mesh, in_specs=in_specs, out_specs=out_specs, check_vma=False
    )
```

```python
import jax
import jax.numpy as jnp
from jax import lax
from jax.experimental import pallas as pl
from jax.experimental.pallas import tpu as pltpu
from jax.sharding import Mesh, PartitionSpec as P

BLK = 128
NB = 8
CAP = 2
VMEM_LIMIT = 24 * 1024 * 1024

SMEM = pl.BlockSpec(memory_space=pltpu.SMEM)
VMEM = pl.BlockSpec(memory_space=pltpu.VMEM)
HBM = pl.BlockSpec(memory_space=pltpu.HBM)

f32 = jnp.float32
bf16 = jnp.bfloat16


def chunk_of(tiles):
    return 48 if tiles % 48 == 0 else (24 if tiles % 24 == 0 else tiles)


def prepare_kernel(
    ids_hbm,
    bias_hbm,
    feats_hbm,
    cot_hbm,
    w_self_hbm,
    w_neigh_hbm,
    slabs_hbm,
    ask_ref,
    bundle_ref,
    slab_ref,
    ids_ref,
    bias_ref,
    sems,
    out_sems,
):
    rows, slab = feats_hbm.shape
    parts = ids_hbm.shape[1]
    hidden = w_self_hbm.shape[1]
    ends = (slab, slab + hidden, slab + 2 * hidden, slab + 2 * hidden + BLK)
    copies = [
        pltpu.make_async_copy(source, target, sems.at[i])
        for i, (source, target) in enumerate(
            (
                (ids_hbm, ids_ref),
                (feats_hbm, slab_ref.at[:, pl.ds(0, slab)]),
                (bias_hbm, bias_ref),
                (feats_hbm, bundle_ref.at[:, pl.ds(0, slab)]),
                (w_self_hbm, bundle_ref.at[:, pl.ds(ends[0], hidden)]),
                (w_neigh_hbm, bundle_ref.at[:, pl.ds(ends[1], hidden)]),
                (cot_hbm.at[:, pl.ds(0, BLK)], bundle_ref.at[:, pl.ds(ends[3], BLK)]),
            )
        )
    ]
    for copy in copies:
        copy.start()
    ask_ref[...] = jnp.zeros_like(ask_ref)
    copies[0].wait()
    ask_ref[:, 0:parts] = ids_ref[...]
    mine = lax.broadcasted_iota(jnp.int32, (rows, BLK), 0) == lax.axis_index("z")
    for c in range(CAP):
        ids = jnp.broadcast_to(ask_ref[c : c + 1, :], (rows, BLK))
        plane = jnp.where(mine, ids, 0).astype(f32).astype(bf16)
        slab_ref[:, slab + c * BLK : slab + (c + 1) * BLK] = plane
    copies[1].wait()
    out_copies = [
        pltpu.make_async_copy(slab_ref, slabs_hbm.at[i], out_sems.at[i])
        for i in range(slabs_hbm.shape[0])
    ]
    for copy in out_copies:
        copy.start()
    copies[2].wait()
    wide = jnp.broadcast_to(bias_ref[...], (rows, rows))
    place = lax.broadcasted_iota(jnp.int32, (rows, rows), 0)
    place = place == lax.broadcasted_iota(jnp.int32, (rows, rows), 1)
    bias = jnp.sum(jnp.where(place, wide, 0.0), axis=1, keepdims=True)
    high = bias.astype(bf16).astype(f32)
    middle = (bias - high).astype(bf16).astype(f32)
    low = bias - high - middle
    lane = lax.broadcasted_iota(jnp.int32, (rows, BLK), 1)
    terms = jnp.where(lane == 0, high, jnp.where(lane == 1, middle, jnp.where(lane == 2, low, 0.0)))
    bundle_ref[:, ends[2] : ends[3]] = terms.astype(bf16)
    for copy in copies[3:] + out_copies:
        copy.wait()


def select_kernel(ask_ref, slabs_hbm, out_ref, slabs_ref, sems):
    along, _, rows, _ = out_ref.shape
    column = slabs_ref.shape[0]
    slab = NB * BLK
    first = lax.axis_index("x") * column
    copies = [
        pltpu.make_async_copy(slabs_hbm.at[k], slabs_ref.at[k], sems.at[k]) for k in range(column)
    ]
    for copy in copies:
        copy.start()
    for k in range(column):
        copies[k].wait()
        for i in range(along):
            for c in range(CAP):
                start = pl.multiple_of(ask_ref[i, c, first + k] * BLK, BLK)
                out_ref[i, k * CAP + c] = slabs_ref[k, :, pl.ds(start, BLK)]
    for c in range(CAP):
        plane = jnp.zeros((rows, BLK), f32)
        for k in range(column):
            plane += slabs_ref[k, :, slab + c * BLK : slab + (c + 1) * BLK].astype(f32)
        for i in range(along):
            out_ref[i, column * CAP + c] = plane.astype(bf16)


def aggregate_kernel(
    dst_hbm,
    counts_hbm,
    cot_hbm,
    fetched_ref,
    adj_ref,
    agg_ref,
    inv_hbm,
    dst_ref,
    counts_ref,
    inv,
    acc_ref,
    small,
):
    along, slots, rows, _ = fetched_ref.shape
    per_row = slots - CAP
    chunk = chunk_of(per_row)
    dst_copy = pltpu.make_async_copy(dst_hbm, dst_ref, small.at[0])
    counts_copy = pltpu.make_async_copy(counts_hbm, counts_ref, small.at[1])
    dst_copy.start()
    counts_copy.start()
    slab = NB * BLK
    cot_copy = pltpu.make_async_copy(
        cot_hbm.at[:, pl.ds(BLK, slab - BLK)], agg_ref.at[:, pl.ds(slab, slab - BLK)], small.at[3]
    )
    cot_copy.start()
    row_ids = lax.broadcasted_iota(jnp.int32, (16, BLK), 0)
    zero = jnp.zeros((rows, BLK), bf16)
    chunks = per_row // chunk
    dst_copy.wait()
    counts_copy.wait()

    acc_ref[...] = jnp.zeros_like(acc_ref)
    ones = jnp.ones((rows, BLK), bf16)

    def step(k, carry):
        products = []
        for i in range(chunk):
            block = fetched_ref[k // chunks, (k % chunks) * chunk + i]
            start = pl.multiple_of((k * chunk + i) * BLK, BLK)
            products.append(jnp.dot(jnp.concatenate([block, ones], axis=0), adj_ref[pl.ds(start, BLK), :], preferred_element_type=f32))
        for i in range(chunk):
            q = k * (chunk // CAP) + i // CAP
            live = (i % CAP) < counts_ref[0, q]
            dst = jnp.where(live, dst_ref[i % CAP, q], NB)
            acc_ref[dst] += products[i][0 : rows + 8]
        return carry

    lax.fori_loop(0, along * chunks, step, 0)
    for n in range(NB):
        inv[n : n + 1] = 1.0 / jnp.maximum(acc_ref[n, rows : rows + 1], 1.0)
    inv_copy = pltpu.make_async_copy(inv, inv_hbm, small.at[2])
    inv_copy.start()
    for n in range(NB):
        part = acc_ref[n, 0:rows] * inv[n : n + 1]
        agg_ref[:, n * BLK : (n + 1) * BLK] = part.astype(bf16)
    inv_copy.wait()
    cot_copy.wait()


def update_kernel(
    dst_hbm,
    counts_hbm,
    inv_hbm,
    agg_ref,
    bundle_hbm,
    adj_ref,
    out_ref,
    self_ref,
    grads_hbm,
    dst_ref,
    counts_ref,
    inv_ref,
    bundle_ref,
    out_all,
    scaled,
    grads_ref,
    out_sems,
    small,
):
    hidden = agg_ref.shape[0]
    slab = NB * BLK
    tiles, rows, _ = grads_ref.shape
    chunk = chunk_of(tiles)
    copies = [
        pltpu.make_async_copy(source, target, small.at[i])
        for i, (source, target) in enumerate(
            (
                (bundle_hbm, bundle_ref),
                (inv_hbm, inv_ref),
                (dst_hbm, dst_ref),
                (counts_hbm, counts_ref),
            )
        )
    ]
    for copy in copies:
        copy.start()
    for copy in copies:
        copy.wait()
    weights = slab
    first = pl.multiple_of(lax.axis_index("feat") * rows, rows)
    w_self = bundle_ref[pl.ds(first, rows), weights : weights + hidden]
    w_neigh = bundle_ref[pl.ds(first, rows), weights + hidden : weights + 2 * hidden]
    tail = bundle_ref[:, weights + 2 * hidden : weights + 2 * hidden + BLK].astype(f32)
    bias = tail[:, 0:1] + tail[:, 1:2] + tail[:, 2:3]
    w_self_all = bundle_ref[:, weights : weights + hidden]
    w_neigh_all = bundle_ref[:, weights + hidden : weights + 2 * hidden]
    contract_rows = (((0,), (0,)), ((), ()))
    width = slab
    for start in range(0, slab, width):
        columns = slice(start, start + width)
        preact = (
            lax.dot_general(
                w_self_all, bundle_ref[:, columns], contract_rows, preferred_element_type=f32
            )
            + lax.dot_general(
                w_neigh_all, agg_ref[:, columns], contract_rows, preferred_element_type=f32
            )
            + bias
        )
        s = 1.0 / (1.0 + jnp.exp(-preact))
        silu = preact * s
        out_all[:, columns] = silu.astype(bf16)
        cotangent = jnp.concatenate(
            [bundle_ref[:, weights + 2 * hidden + BLK :], agg_ref[:, slab:]], axis=1
        ).astype(f32)
        d_preact = (cotangent * (s + silu * (1.0 - s))).astype(bf16)
        self_ref[:, columns] = jnp.dot(w_self, d_preact, preferred_element_type=f32)
        neigh = jnp.dot(w_neigh, d_preact, preferred_element_type=f32)
        for half in range(width // BLK):
            n = start // BLK + half
            part = neigh[:, half * BLK : (half + 1) * BLK] * inv_ref[n : n + 1]
            scaled[n] = part.astype(bf16)
    out_ref[...] = out_all[pl.ds(first, rows), :]

    zero = jnp.zeros((rows, BLK), bf16)
    contract_columns = (((1,), (1,)), ((), ()))

    def grads_copy(k):
        part = pl.ds(k * chunk, chunk)
        return pltpu.make_async_copy(grads_ref.at[part], grads_hbm.at[part], out_sems.at[k])

    def step(k, carry):
        for i in range(chunk):
            t = k * chunk + i
            q = k * (chunk // CAP) + i // CAP
            live = (i % CAP) < counts_ref[0, q]
            chosen = jnp.where(live, scaled[dst_ref[i % CAP, q]], zero)
            start = pl.multiple_of(t * BLK, BLK)
            grads = lax.dot_general(
                chosen, adj_ref[pl.ds(start, BLK), :], contract_columns, preferred_element_type=f32
            )
            grads_ref[t] = grads.astype(bf16)
        grads_copy(k).start()
        return carry

    lax.fori_loop(0, tiles // chunk, step, 0)
    for k in range(tiles // chunk):
        grads_copy(k).wait()


def sum_kernel(ids_ref, grads_ref, self_hbm, out_ref, self_ref, sums, sem):
    self_copy = pltpu.make_async_copy(self_hbm, self_ref, sem)
    self_copy.start()
    tiles, rows, _ = grads_ref.shape
    along = ids_ref.shape[0]
    column = tiles // (along * CAP)
    sums[...] = jnp.zeros_like(sums)
    for q in range(tiles // CAP):
        for c in range(CAP):
            block = grads_ref[q * CAP + c].astype(f32)
            sums[c, ids_ref[q // column, c, q % column]] += block
    self_copy.wait()
    for n in range(NB):
        columns = slice(n * BLK, (n + 1) * BLK)
        total = self_ref[:, columns]
        for c in range(CAP):
            total += sums[c, n]
        out_ref[:, columns] = total


def params(limit=VMEM_LIMIT):
    return pltpu.CompilerParams(vmem_limit_bytes=limit)


def shape(dims, dtype):
    return jax.ShapeDtypeStruct(dims, dtype)


def prepare(block_ids, bias, feats, cotangent, w_self, w_neigh, receivers):
    rows, slab = feats.shape
    hidden = w_self.shape[1]
    return pl.pallas_call(
        prepare_kernel,
        out_shape=(
            shape((receivers, rows, slab + CAP * BLK), bf16),
            shape((CAP, BLK), jnp.int32),
            shape((rows, slab + 2 * hidden + 2 * BLK), bf16),
        ),
        in_specs=[HBM] * 6,
        out_specs=(HBM, VMEM, VMEM),
        scratch_shapes=[
            pltpu.VMEM((rows, slab + CAP * BLK), bf16),
            pltpu.VMEM(block_ids.shape, jnp.int32),
            pltpu.VMEM((1, rows), f32),
            pltpu.SemaphoreType.DMA((7,)),
            pltpu.SemaphoreType.DMA((receivers,)),
        ],
        compiler_params=params(66_800_000),
        name="prepare",
    )(block_ids, bias, feats, cotangent, w_self, w_neigh)


def select(asked, slabs, along):
    column, rows, _ = slabs.shape
    return pl.pallas_call(
        select_kernel,
        out_shape=shape((along, column * CAP + CAP, rows, BLK), bf16),
        in_specs=[SMEM, HBM],
        out_specs=VMEM,
        scratch_shapes=[
            pltpu.VMEM(slabs.shape, bf16),
            pltpu.SemaphoreType.DMA((column,)),
        ],
        compiler_params=params(),
        name="select_blocks",
    )(asked, slabs)


def aggregate(dst, counts, cotangent, fetched, adj):
    along, slots, rows, _ = fetched.shape
    tiles = along * (slots - CAP)
    return pl.pallas_call(
        aggregate_kernel,
        out_shape=(shape((rows, (2 * NB - 1) * BLK), bf16), shape((NB, BLK), f32)),
        in_specs=[HBM, HBM, HBM, VMEM, VMEM],
        out_specs=(VMEM, HBM),
        scratch_shapes=[
            pltpu.SMEM(dst.shape, jnp.int32),
            pltpu.SMEM(counts.shape, jnp.int32),
            pltpu.VMEM((NB, BLK), f32),
            pltpu.VMEM((NB + 1, rows + 8, BLK), f32),
            pltpu.SemaphoreType.DMA((4,)),
        ],
        compiler_params=params(),
        name="aggregate",
    )(dst, counts, cotangent, fetched, adj)


def update(dst, counts, inverse, agg, bundle, adj, rows):
    hidden, slab = agg.shape[0], NB * BLK
    tiles = adj.shape[0] // BLK
    return pl.pallas_call(
        update_kernel,
        out_shape=(
            shape((rows, slab), bf16),
            shape((rows, slab), f32),
            shape((tiles, rows, BLK), bf16),
        ),
        in_specs=[HBM] * 3 + [VMEM, HBM, VMEM],
        out_specs=(VMEM, VMEM, HBM),
        scratch_shapes=[
            pltpu.SMEM(dst.shape, jnp.int32),
            pltpu.SMEM(counts.shape, jnp.int32),
            pltpu.VMEM((NB, BLK), f32),
            pltpu.VMEM(bundle.shape, bf16),
            pltpu.VMEM((hidden, slab), bf16),
            pltpu.VMEM((NB, rows, BLK), bf16),
            pltpu.VMEM((tiles, rows, BLK), bf16),
            pltpu.SemaphoreType.DMA((tiles // chunk_of(tiles),)),
            pltpu.SemaphoreType.DMA((4,)),
        ],
        compiler_params=params(),
        name="update",
    )(dst, counts, inverse, agg, bundle, adj)


def sum_returned(ids, returned, self_grad):
    return pl.pallas_call(
        sum_kernel,
        out_shape=shape(self_grad.shape, f32),
        in_specs=[SMEM, VMEM, HBM],
        out_specs=VMEM,
        scratch_shapes=[
            pltpu.VMEM(self_grad.shape, f32),
            pltpu.VMEM((CAP, NB, returned.shape[1], BLK), f32),
            pltpu.SemaphoreType.DMA,
        ],
        compiler_params=params(),
        name="sum_returned",
    )(ids, returned, self_grad)


def per_device(feats, w_self, w_neigh, bias, cotangent, block_ids, req_counts, tile_dst, adjacency):
    along, column = lax.axis_size("x"), lax.axis_size("z")
    graph_parts = along * column
    rows, slab = feats.shape
    tiles = graph_parts * CAP
    per_row = column * CAP
    adj = adjacency.reshape(tiles * BLK, BLK)
    dst = tile_dst[0].T

    slabs, ask, bundle = prepare(
        block_ids[0].T, bias.reshape(1, rows), feats, cotangent, w_self, w_neigh, column
    )
    slabs = lax.all_to_all(slabs, "z", 0, 0)
    asked = lax.all_gather(ask, "x", axis=0)
    bundle = lax.all_gather(bundle, "feat", axis=0, tiled=True)
    slabs, asked, bundle = lax.optimization_barrier((slabs, asked, bundle))
    picked = select(asked, slabs, along)
    fetched = lax.all_to_all(picked, "x", 0, 0)
    agg, inverse = aggregate(dst, req_counts, cotangent, fetched, adj)
    agg_all = lax.all_gather(agg, "feat", axis=0, tiled=True)
    output, self_grad, grads = update(
        dst, req_counts, inverse, agg_all, bundle, adj, rows
    )
    returned = lax.all_to_all(
        grads.reshape(graph_parts, CAP, rows, BLK), ("x", "z"), 0, 0
    ).reshape(tiles, rows, BLK)
    me = lax.axis_index("x") * column + lax.axis_index("z")
    ids = lax.dynamic_slice(fetched, (0, per_row, 0, me), (along, CAP, rows, 1))
    ids = ids.reshape(along, CAP, rows).astype(jnp.int32)
    feat_grad = sum_returned(ids, returned, self_grad)
    return (output, feat_grad)


def solution(mesh):
    graph, feat = mesh.devices.shape
    along = 4 if graph % 12 == 0 else 2
    mesh = Mesh(mesh.devices.reshape(along, graph // along, feat), ("x", "z", "feat"))
    graph = ("x", "z")
    in_specs = (
        P("feat", graph),
        P("feat", None),
        P("feat", None),
        P("feat"),
        P("feat", graph),
        P(graph, None, None),
        P(graph, None),
        P(graph, None, None),
        P(graph, None, None, None, None),
    )
    out_specs = (P("feat", graph), P("feat", graph))
    return jax.shard_map(
        per_device, mesh=mesh, in_specs=in_specs, out_specs=out_specs, check_vma=False
    )
```
